32 devices in a mesh: pipe: 2 (over core), dp: 4 (over z), seq: 4 (over y, x).
Axes of the slice: x: 2, y: 2, z: 4, core: 2. Of those that a mesh axis runs over, the one named last changes fastest.
Arguments:
- tokens: bfloat16 [16, 512, 768], P('dp', 'seq'), may hold values from -6 to 6
- cotangent: bfloat16 [16, 512, 768], P('dp', 'seq'), may hold values from -6 to 6
- lengths: int32 [16, 4], P('dp'), may hold values from 1 to 509, as said below
- norm_params: float32 [2, 4, 768], P('pipe'), may hold values from -1 to 1.5, as said below
- qkv_weight: bfloat16 [2, 768, 2304], P('pipe'), may hold values from -0.21875 to 0.21875
- feature_weight: bfloat16 [2, 64, 1536], P('pipe'), may hold values from -0.75 to 0.75
- out_weight: bfloat16 [2, 768, 768], P('pipe'), may hold values from -0.875 to 0.875
- up_weight: bfloat16 [2, 768, 3072], P('pipe'), may hold values from -0.21875 to 0.21875
- down_weight: bfloat16 [2, 3072, 768], P('pipe'), may hold values from -0.109375 to 0.109375
Outputs:
- layer_outputs: bfloat16 [2, 16, 512, 768], P('pipe', 'dp', 'seq')
- input_grads: bfloat16 [2, 16, 512, 768], P('pipe', 'dp', 'seq')
- grad_norms: float32 [2, 4, 768], P('pipe', None, ('dp', 'seq'))
- grad_querykey: float32 [2, 768, 1536], P('pipe', None, ('dp', 'seq'))
- grad_value: float32 [2, 768, 768], P('pipe', None, ('dp', 'seq'))
- grad_features: float32 [2, 64, 1536], P('pipe', None, ('dp', 'seq'))
- grad_out: float32 [2, 768, 768], P('pipe', None, ('dp', 'seq'))
- grad_up: float32 [2, 768, 3072], P('pipe', None, ('dp', 'seq'))
- grad_down: float32 [2, 3072, 768], P('pipe', None, ('dp', 'seq'))
The draws below stay inside these ranges and needn't reach their ends.
Inputs may be any that keep to these rules, and one draw needn't show every extreme that they name: Each row is one micro-batch: 4 document lengths in order, summing to 512. In each group of 4 rows (one index of dp), one row, the same offset in every group and drawn from the seed, has one document of exactly 509 positions, preceded and followed by documents of one position; no document of any row is longer. `norm_params`: rows 0 and 2 of each layer are gains, rows 1 and 3 shifts.
All inputs are finite; a program needn't handle non-finite values.
Results may differ from the reference program's by a relative error of at most 0.013.
Values may be sent and summed in bfloat16 or wider, within the bound.
No kernel may reach another device: no remote copies, remote signals or barrier semaphores. Data moves between devices by JAX's collectives and lax.ppermute only.
A program may use at most 320 MiB of HBM per device.

```python
import jax
import jax.numpy as jnp
from jax import lax

D = 768
H = 12
HD = 64
FF = 3072
CH = 64
NDOCS = 4
MICRO = 4
LEN = 512
NB = 16
N_PIPE = 2


def draw_lengths(key, part):
    key = jax.random.fold_in(key, 11)
    row_keys = jax.random.split(key, NB + 1)
    picked = jax.random.randint(row_keys[0], (), 0, MICRO)
    head_count = NDOCS // 2
    tail_count = NDOCS - 1 - head_count
    head_cuts = jnp.arange(1, head_count + 1, dtype=jnp.int32)
    tail_cuts = LEN - tail_count + jnp.arange(tail_count, dtype=jnp.int32)
    near_cuts = jnp.concatenate([head_cuts, tail_cuts])

    def one_row(row_key, row_index):
        spread_cuts = jnp.sort(jax.random.permutation(row_key, LEN - 1)[:NDOCS - 1] + 1)
        cuts = jnp.where(row_index % MICRO == picked, near_cuts, spread_cuts).astype(jnp.int32)
        edges = jnp.concatenate([jnp.zeros((1,), jnp.int32), cuts, jnp.full((1,), LEN, jnp.int32)])
        return edges[1:] - edges[:-1]
    return jax.vmap(one_row)(row_keys[1:], jnp.arange(NB, dtype=jnp.int32))


def draw_norm_params(key, part):
    key = jax.random.fold_in(key, 7)
    gain_key, shift_key = jax.random.split(key)
    gains = jax.random.uniform(gain_key, (N_PIPE, 2, 1, D), jnp.float32, 0.6, 1.4)
    shifts = jnp.clip(0.3 * jax.random.normal(shift_key, (N_PIPE, 2, 1, D), jnp.float32), -1.0, 1.0)
    return jnp.concatenate([gains, shifts], 2).reshape(N_PIPE, 4, D)


def shard_levels(key, dims, shards, smallest, top_value):
    def one(dim, shards_of):
        draws = jax.random.uniform(jax.random.fold_in(jax.random.fold_in(key, 6), dim), (shards_of,), jnp.float32, smallest / len(shards), top_value / len(shards))
        return jnp.repeat(jnp.exp(draws), dims[dim] // shards_of).reshape((-1,) + (1,) * (len(dims) - dim - 1))

    gain = one(*shards[0])
    for cut in shards[1:]:
        gain = gain * one(*cut)
    return gain


def scatter_about(stream_key, extent, scale, reach, cuts=(), kind=jnp.bfloat16):
    drawn = jax.random.normal(stream_key, extent, jnp.float32) * scale
    if len(cuts) > 0:
        drawn = shard_levels(stream_key, extent, cuts, -0.22, 0.18) * drawn
    return jnp.clip(drawn, min=-reach, max=reach).astype(kind)


def setup_inputs(seed: int = 0) -> dict:
    key_of = jax.random.split(jax.random.key(seed), 10)
    tokens = scatter_about(key_of[0], (NB, LEN, D), 1.0, 6.0, ((0, 4), (1, 4)))
    cotangent = scatter_about(key_of[1], (NB, LEN, D), 1.0, 6.0, ((0, 4), (1, 4)))
    lengths = draw_lengths(jax.random.fold_in(key_of[9], 71), 0)
    norm_params = draw_norm_params(jax.random.fold_in(key_of[9], 71), 0)
    qkv_weight = scatter_about(key_of[4], (N_PIPE, D, 3 * D), D ** -0.5, 0.21875, ((0, 2),))
    feature_weight = scatter_about(key_of[5], (N_PIPE, HD, 2 * D), HD ** -0.5, 0.75, ((0, 2),))
    out_weight = scatter_about(key_of[6], (N_PIPE, D, D), (D // 16) ** -0.5, 0.875, ((0, 2),))
    up_weight = scatter_about(key_of[7], (N_PIPE, D, FF), D ** -0.5, 0.21875, ((0, 2),))
    down_weight = scatter_about(key_of[8], (N_PIPE, FF, D), FF ** -0.5, 0.109375, ((0, 2),))
    return dict(tokens=tokens, cotangent=cotangent, lengths=lengths, norm_params=norm_params, qkv_weight=qkv_weight, feature_weight=feature_weight, out_weight=out_weight, up_weight=up_weight, down_weight=down_weight)


highest = lax.Precision.HIGHEST

@jax.custom_vjp
def low(v):
    return lax.optimization_barrier(v.astype(jnp.bfloat16)).astype(jnp.float32)

@jax.custom_vjp
def low_back(v):
    return v

def low_keep(v):
    return (low(v), None)

def low_pass(kept, grad):
    return (grad,)

def back_keep(v):
    return (v, None)

def back_low(kept, grad):
    return (low(grad),)
low.defvjp(low_keep, low_pass)
low_back.defvjp(back_keep, back_low)

def normalize(stream, norm_gain, norm_shift):
    centred = stream - lax.optimization_barrier(jnp.mean(stream, -1, keepdims=True))
    spread = lax.optimization_barrier(jnp.mean(centred * centred, -1, keepdims=True))
    return centred * lax.rsqrt(spread + 1e-05) * norm_gain + norm_shift

def features(logits):
    return jnp.concatenate([jax.nn.softmax(logits, -1), jax.nn.softmax(-logits, -1)], -1)

def smooth(hidden_pre):
    return jax.nn.gelu(hidden_pre, approximate=True)

def segments(lengths_row, positions):
    doc_ends = jnp.cumsum(lengths_row).astype(jnp.int32)
    return lax.optimization_barrier(jnp.sum((doc_ends[None, :] <= positions[:, None]).astype(jnp.int32), 1))

def span_step(carried_in, block_in):
    kv_state, norm_state, last_seg = carried_in
    query_feats, key_feats, values, seg_ids = block_in
    seg_float = seg_ids.astype(jnp.float32)
    scores = jnp.einsum('thf,shf->hts', query_feats, key_feats, precision=highest)
    places = jnp.arange(CH, dtype=jnp.int32)
    allowed = (places[:, None] >= places[None, :]) & (seg_ids[:, None] == seg_ids[None, :])
    weights = jnp.where(allowed[None], scores, 0.0)
    carried = (seg_float == last_seg).astype(jnp.float32)
    numerator = jnp.einsum('hts,shd->thd', weights, values, precision=highest) + carried[:, None, None] * jnp.einsum('thf,hfd->thd', query_feats, kv_state, precision=highest)
    denominator = lax.optimization_barrier(jnp.sum(weights, -1)).T + carried[:, None] * jnp.einsum('thf,hf->th', query_feats, norm_state, precision=highest)
    tail_seg = seg_float[-1]
    inside = (seg_float == tail_seg).astype(jnp.float32)
    kept_part = (last_seg == tail_seg).astype(jnp.float32)
    tail_keys = key_feats * inside[:, None, None]
    kv_state = kept_part * kv_state + jnp.einsum('shf,shd->hfd', tail_keys, values, precision=highest)
    norm_state = kept_part * norm_state + lax.optimization_barrier(jnp.sum(tail_keys, 0))
    return ((kv_state, norm_state, tail_seg), numerator / denominator[:, :, None])

def attend(query_feats, key_feats, values, seg_ids):
    row_count = query_feats.shape[0]
    block_count = row_count // CH
    blocks = (query_feats.reshape(block_count, CH, H, 2 * HD), key_feats.reshape(block_count, CH, H, 2 * HD), values.reshape(block_count, CH, H, HD), seg_ids.reshape(block_count, CH))
    start = (jnp.zeros((H, 2 * HD, HD), jnp.float32), jnp.zeros((H, 2 * HD), jnp.float32), jnp.float32(-1.0))
    closing, mixed_out = lax.scan(jax.checkpoint(span_step), start, blocks)
    return mixed_out.reshape(row_count, H, HD)

def layer(stream, weights, which, seg_ids):
    norm_rows = weights[0][which]
    w_qkv = weights[1][which]
    w_feat = weights[2][which]
    w_out = weights[3][which]
    w_up = weights[4][which]
    w_down = weights[5][which]
    row_count = stream.shape[0]
    normed = low(normalize(stream, norm_rows[0], norm_rows[1]))
    joined = low_back(jnp.dot(normed, w_qkv, precision=highest))
    queries = low(joined[:, :D]).reshape(row_count, H, HD)
    key_rows = low(joined[:, D:2 * D]).reshape(row_count, H, HD)
    values = joined[:, 2 * D:].reshape(row_count, H, HD)
    feat_maps = w_feat.reshape(HD, 2, H, HD)
    q_logit = low_back(jnp.einsum('shd,dhe->she', queries, feat_maps[:, 0], precision=highest))
    k_logit = low_back(jnp.einsum('shd,dhe->she', key_rows, feat_maps[:, 1], precision=highest))
    mixed_out = attend(features(q_logit), features(k_logit), values, seg_ids)
    branch = low_back(jnp.dot(low(mixed_out.reshape(row_count, D)), w_out, precision=highest))
    middle = stream + branch
    normed_two = low(normalize(middle, norm_rows[2], norm_rows[3]))
    hidden_pre = low_back(jnp.dot(normed_two, w_up, precision=highest))
    hidden = low(smooth(hidden_pre))
    return middle + low_back(jnp.dot(hidden, w_down, precision=highest))

def reference(tokens, cotangent, lengths, norm_params, qkv_weight, feature_weight, out_weight, up_weight, down_weight):
    params = (norm_params.astype(jnp.float32), qkv_weight.astype(jnp.float32), feature_weight.astype(jnp.float32), out_weight.astype(jnp.float32), up_weight.astype(jnp.float32), down_weight.astype(jnp.float32))
    positions = jnp.arange(LEN, dtype=jnp.int32)

    def one_batch(totals, batch_in):
        tok_rows, cot_rows, lengths_row = batch_in
        seg_ids = segments(lengths_row, positions)
        stream = tok_rows.astype(jnp.float32)
        bump_zero = jnp.zeros_like(stream)

        def forward(stream_in, weights, bump_in):
            first_out = layer(stream_in, weights, 0, seg_ids)
            second = layer(low(low_back(first_out)) + bump_in, weights, 1, seg_ids)
            return (first_out, second)
        (first_out, second), pullback = jax.vjp(forward, stream, params, bump_zero)
        grad_stream, grad_weights, grad_bump = pullback((jnp.zeros_like(first_out), cot_rows.astype(jnp.float32)))
        totals = jax.tree.map(jnp.add, totals, grad_weights)
        return (totals, (first_out.astype(jnp.bfloat16), second.astype(jnp.bfloat16), grad_stream.astype(jnp.bfloat16), grad_bump.astype(jnp.bfloat16)))
    zero_grads = jax.tree.map(jnp.zeros_like, params)
    totals, outputs = lax.scan(one_batch, zero_grads, (tokens, cotangent, lengths))
    first_all, second_all, grad_first, grad_second = outputs
    grad_qkv = totals[1]
    return (jnp.stack([first_all, second_all]), jnp.stack([grad_first, grad_second]), totals[0], grad_qkv[:, :, :2 * D], grad_qkv[:, :, 2 * D:], totals[2], totals[3], totals[4], totals[5])
```

```python
import functools
from typing import Any, NamedTuple

import jax
import jax.numpy as jnp
from jax import lax
from jax.experimental import pallas as pl
from jax.experimental.pallas import tpu as pltpu
from jax.sharding import PartitionSpec as P

D = 768
H = 12
HD = 64
CH = 64


highest = lax.Precision.HIGHEST
bfloat = jnp.bfloat16
single = jnp.float32


def carried_in_2(value, axis, join, neutral, backward):
    count, mine = (lax.axis_size(axis), lax.axis_index(axis))
    pieces = jax.tree.map(lambda part: lax.all_gather(part, axis), value)
    if backward:
        pieces = jax.tree.map(lambda part: part[::-1], pieces)
        mine = count - 1 - mine
    total = jax.tree.map(
        lambda part, zero: jnp.full_like(part, 0) + jnp.asarray(zero, part.dtype), value, neutral
    )

    def lap(position, total):
        longer = join(total, jax.tree.map(lambda part: part[position], pieces))
        return jax.tree.map(lambda new, old: jnp.where(position < mine, new, old), longer, total)

    return lax.fori_loop(0, count - 1, lap, total)


def for_sending(shard):
    return jax.tree.map(lambda a: a.astype(jnp.bfloat16) if a.dtype == jnp.float32 else a, shard)


def passed_along(shard, axis, by):
    length = lax.axis_size(axis)
    pairs = [(i, i + by) for i in range(length) if 0 <= i + by < length]
    return lax.ppermute(shard, axis, pairs)


def normalize(stream, norm_gain, norm_shift):
    centred = stream - jnp.mean(stream, -1, keepdims=True)
    spread = jnp.mean(centred * centred, -1, keepdims=True)
    return centred * lax.rsqrt(spread + 1e-05) * norm_gain + norm_shift


def features(logits):
    return jnp.concatenate([jax.nn.softmax(logits, -1), jax.nn.softmax(-logits, -1)], -1)


def flat_features(flat_logits):
    row_count = flat_logits.shape[0]
    return features(flat_logits.reshape(row_count, H, HD)).reshape(row_count, 2 * D)


def smooth(hidden_pre):
    return jax.nn.gelu(hidden_pre, approximate=True)


def segments(lengths_row, positions):
    doc_ends = jnp.cumsum(lengths_row)
    return jnp.sum((doc_ends[None, :] <= positions[:, None]).astype(jnp.int32), 1)


def span_step(carried_in, block_in):
    kv_state, norm_state, last_seg = carried_in
    query_feats, key_feats, values, seg_ids = block_in
    seg_float = seg_ids.astype(single)
    scores = jnp.einsum("thf,shf->hts", query_feats, key_feats, precision=highest)
    places = jnp.arange(CH, dtype=jnp.int32)
    allowed = (places[:, None] >= places[None, :]) & (seg_ids[:, None] == seg_ids[None, :])
    weights = jnp.where(allowed[None], scores, 0.0)
    carried = (seg_float == last_seg).astype(single)
    numerator = jnp.einsum("hts,shd->thd", weights, values, precision=highest) + carried[
        :, None, None
    ] * jnp.einsum("thf,hfd->thd", query_feats, kv_state, precision=highest)
    denominator = jnp.sum(weights, -1).T + carried[:, None] * jnp.einsum(
        "thf,hf->th", query_feats, norm_state, precision=highest
    )
    tail_seg = seg_float[-1]
    inside = (seg_float == tail_seg).astype(single)
    kept_part = (last_seg == tail_seg).astype(single)
    tail_keys = key_feats * inside[:, None, None]
    kv_state = kept_part * kv_state + jnp.einsum(
        "shf,shd->hfd", tail_keys, values, precision=highest
    )
    norm_state = kept_part * norm_state + jnp.sum(tail_keys, 0)
    return ((kv_state, norm_state, tail_seg), numerator / denominator[:, :, None])


def attend(query_feats, key_feats, values, seg_ids, kv_state, norm_state, last_seg):
    row_count = query_feats.shape[0]
    block_count = row_count // CH
    blocks = (
        query_feats.reshape(block_count, CH, H, 2 * HD),
        key_feats.reshape(block_count, CH, H, 2 * HD),
        values.reshape(block_count, CH, H, HD),
        seg_ids.reshape(block_count, CH),
    )
    closing, mixed_out = lax.scan(span_step, (kv_state, norm_state, last_seg), blocks)
    return mixed_out.reshape(row_count, H, HD)


def tail_state(key_feats, values, seg_ids):
    row_count = key_feats.shape[0]
    key_three = key_feats.reshape(row_count, H, 2 * HD)
    value_three = values.reshape(row_count, H, HD)
    seg_float = seg_ids.astype(single)
    tail_seg = seg_float[-1]
    tail_keys = key_three * (seg_float == tail_seg).astype(single)[:, None, None]
    return (
        jnp.einsum("shf,shd->hfd", tail_keys, value_three, precision=highest),
        jnp.sum(tail_keys, 0),
        tail_seg,
    )


def join_states(earlier, later):
    early_kv, early_norm, early_seg = earlier
    late_kv, late_norm, late_seg = later
    is_blank = late_seg < 0.0
    matches = early_seg == late_seg
    kv_sum = jnp.where(is_blank, early_kv, late_kv + jnp.where(matches, early_kv, 0.0))
    norm_sum = jnp.where(is_blank, early_norm, late_norm + jnp.where(matches, early_norm, 0.0))
    return (kv_sum, norm_sum, jnp.where(is_blank, early_seg, late_seg))


def empty_state():
    return (jnp.zeros((H, 2 * HD, HD), single), jnp.zeros((H, 2 * HD), single), jnp.float32(-1.0))


class Front(NamedTuple):
    stream: Any
    normed: Any
    queries: Any
    key_rows: Any
    values: Any
    q_logit: Any
    k_logit: Any
    query_feats: Any
    key_feats: Any


class Complete(NamedTuple):
    stream: Any
    normed: Any
    queries: Any
    key_rows: Any
    values: Any
    q_logit: Any
    k_logit: Any
    query_feats: Any
    key_feats: Any
    incoming_kv: Any
    incoming_norm: Any
    incoming_seg: Any
    mixed_low: Any
    middle: Any
    normed_two: Any
    hidden_pre: Any
    hidden: Any
    result: Any


def front_pass(section_input, params):
    norm_rows, w_qkv, w_feat = (params[0], params[1], params[2])
    stream = section_input.astype(single)
    row_count = stream.shape[0]
    normed = normalize(stream, norm_rows[0], norm_rows[1]).astype(bfloat)
    joined = jnp.dot(normed, w_qkv, preferred_element_type=single)
    queries = joined[:, :D].astype(bfloat)
    key_rows = joined[:, D : 2 * D].astype(bfloat)
    values = joined[:, 2 * D :]
    feat_maps = w_feat.reshape(HD, 2, H, HD)
    q_logit = jnp.einsum(
        "shd,dhe->she",
        queries.reshape(row_count, H, HD),
        feat_maps[:, 0],
        preferred_element_type=single,
    ).reshape(row_count, D)
    k_logit = jnp.einsum(
        "shd,dhe->she",
        key_rows.reshape(row_count, H, HD),
        feat_maps[:, 1],
        preferred_element_type=single,
    ).reshape(row_count, D)
    return Front(
        stream=stream,
        normed=normed,
        queries=queries,
        key_rows=key_rows,
        values=values,
        q_logit=q_logit,
        k_logit=k_logit,
        query_feats=flat_features(q_logit),
        key_feats=flat_features(k_logit),
    )


def rear_pass(front, incoming, seg_ids, params):
    norm_rows, w_out, w_up, w_down = (params[0], params[3], params[4], params[5])
    stream = front.stream
    row_count = stream.shape[0]
    mixed_out = attend(
        front.query_feats,
        front.key_feats,
        front.values,
        seg_ids,
        incoming[0],
        incoming[1],
        incoming[2],
    )
    mixed_low = mixed_out.reshape(row_count, D).astype(bfloat)
    middle = stream + jnp.dot(mixed_low, w_out, preferred_element_type=single)
    normed_two = normalize(middle, norm_rows[2], norm_rows[3]).astype(bfloat)
    hidden_pre = jnp.dot(normed_two, w_up, preferred_element_type=single)
    hidden = smooth(hidden_pre).astype(bfloat)
    result = middle + jnp.dot(hidden, w_down, preferred_element_type=single)
    return Complete(
        *front,
        incoming_kv=incoming[0],
        incoming_norm=incoming[1],
        incoming_seg=incoming[2],
        mixed_low=mixed_low,
        middle=middle,
        normed_two=normed_two,
        hidden_pre=hidden_pre,
        hidden=hidden,
        result=result,
    )


def backward_pass(complete, grad_result, seg_ids, params):
    norm_rows, w_qkv, w_feat, w_out, w_up, w_down = params
    row_count = grad_result.shape[0]
    down_grad = grad_result.astype(bfloat)
    grad_down = jnp.einsum(
        "sf,sd->fd", complete.hidden, down_grad, preferred_element_type=single
    )
    grad_hidden = jnp.einsum("sd,fd->sf", down_grad, w_down, preferred_element_type=single)
    unused, smooth_back = jax.vjp(smooth, complete.hidden_pre)
    pre_grad = smooth_back(grad_hidden)[0].astype(bfloat)
    grad_up = jnp.einsum(
        "sd,sf->df", complete.normed_two, pre_grad, preferred_element_type=single
    )
    grad_normed_two = jnp.einsum("sf,df->sd", pre_grad, w_up, preferred_element_type=single)
    unused, norm_back_two = jax.vjp(normalize, complete.middle, norm_rows[2], norm_rows[3])
    grad_middle, grad_gain_two, grad_shift_two = norm_back_two(grad_normed_two)
    grad_middle = grad_middle + grad_result
    branch_grad = grad_middle.astype(bfloat)
    grad_out = jnp.einsum(
        "sa,sd->ad", complete.mixed_low, branch_grad, preferred_element_type=single
    )
    grad_mixed = jnp.einsum("sd,ad->sa", branch_grad, w_out, preferred_element_type=single).reshape(
        row_count, H, HD
    )
    last_seg = complete.incoming_seg

    def core_attend(query_feats, key_feats, values, kv_state, norm_state):
        return attend(query_feats, key_feats, values, seg_ids, kv_state, norm_state, last_seg)

    unused, core_back = jax.vjp(
        core_attend,
        complete.query_feats,
        complete.key_feats,
        complete.values,
        complete.incoming_kv,
        complete.incoming_norm,
    )
    grad_qf, grad_kf, grad_values, grad_kv, grad_norm = core_back(grad_mixed)
    passed = carried_in_2((grad_kv, grad_norm, last_seg), "seq", join_states, empty_state(), True)

    def summary(key_feats, values):
        kv_sum, norm_sum, tail_seg = tail_state(key_feats, values, seg_ids)
        return (kv_sum, norm_sum)

    unused, summary_back = jax.vjp(summary, complete.key_feats, complete.values)
    extra_kf, extra_values = summary_back((passed[0], passed[1]))
    grad_kf = grad_kf + extra_kf
    grad_values = grad_values + extra_values
    unused, feat_back_q = jax.vjp(flat_features, complete.q_logit)
    unused, feat_back_k = jax.vjp(flat_features, complete.k_logit)
    q_logit_grad = feat_back_q(grad_qf)[0].astype(bfloat).reshape(row_count, H, HD)
    k_logit_grad = feat_back_k(grad_kf)[0].astype(bfloat).reshape(row_count, H, HD)
    feat_maps = w_feat.reshape(HD, 2, H, HD)
    grad_map_q = jnp.einsum(
        "shd,she->dhe",
        complete.queries.reshape(row_count, H, HD),
        q_logit_grad,
        preferred_element_type=single,
    )
    grad_map_k = jnp.einsum(
        "shd,she->dhe",
        complete.key_rows.reshape(row_count, H, HD),
        k_logit_grad,
        preferred_element_type=single,
    )
    grad_queries = jnp.einsum(
        "she,dhe->shd", q_logit_grad, feat_maps[:, 0], preferred_element_type=single
    )
    grad_keys = jnp.einsum(
        "she,dhe->shd", k_logit_grad, feat_maps[:, 1], preferred_element_type=single
    )
    joined_grad = jnp.concatenate(
        [
            grad_queries.reshape(row_count, D),
            grad_keys.reshape(row_count, D),
            grad_values.reshape(row_count, D),
        ],
        1,
    ).astype(bfloat)
    grad_qkv = jnp.einsum(
        "sd,se->de", complete.normed, joined_grad, preferred_element_type=single
    )
    grad_normed = jnp.einsum("se,de->sd", joined_grad, w_qkv, preferred_element_type=single)
    unused, norm_back_one = jax.vjp(normalize, complete.stream, norm_rows[0], norm_rows[1])
    grad_stream, grad_gain_one, grad_shift_one = norm_back_one(grad_normed)
    grad_norms = jnp.stack([grad_gain_one, grad_shift_one, grad_gain_two, grad_shift_two])
    grad_maps = jnp.stack([grad_map_q, grad_map_k], 1).reshape(HD, 2 * D)
    return (
        grad_stream + grad_middle,
        (grad_norms, grad_qkv, grad_maps, grad_out, grad_up, grad_down),
    )


def general_on_device(
    tokens,
    cotangent,
    lengths,
    norm_params,
    qkv_weight,
    feature_weight,
    out_weight,
    up_weight,
    down_weight,
):
    params = (
        norm_params[0],
        qkv_weight[0],
        feature_weight[0],
        out_weight[0],
        up_weight[0],
        down_weight[0],
    )
    section_id = lax.axis_index("pipe")
    micro_count = tokens.shape[0]
    row_count = tokens.shape[1]
    positions = lax.axis_index("seq") * row_count + jnp.arange(row_count, dtype=jnp.int32)
    received = jnp.zeros((row_count, D), bfloat)
    kept_list = []
    sent_list = []
    for moment in range(micro_count + 1):
        micro_index = jnp.clip(moment - section_id, 0, micro_count - 1)
        own_rows = lax.dynamic_index_in_dim(tokens, micro_index, 0, False)
        section_input = jnp.where(section_id == 0, own_rows, received)
        seg_ids = segments(lax.dynamic_index_in_dim(lengths, micro_index, 0, False), positions)
        front = front_pass(section_input, params)
        local_state = tail_state(front.key_feats, front.values, seg_ids)
        incoming = carried_in_2(local_state, "seq", join_states, empty_state(), False)
        complete = rear_pass(front, incoming, seg_ids, params)
        kept_list.append(complete)
        sent_value = complete.result.astype(bfloat)
        sent_list.append(sent_value)
        if moment < micro_count:
            received = passed_along(for_sending(sent_value), "pipe", 1).astype(sent_value.dtype)
    totals = tuple((jnp.zeros(tensor.shape, single) for tensor in params))
    returned = jnp.zeros((row_count, D), bfloat)
    back_list = []
    is_first = section_id == 0
    for moment in range(micro_count + 1):
        raw_index = moment - 1 + section_id
        micro_index = jnp.clip(raw_index, 0, micro_count - 1)
        active = (raw_index >= 0) & (raw_index < micro_count)
        own_grad = lax.dynamic_index_in_dim(cotangent, micro_index, 0, False)
        grad_result = jnp.where(section_id == 1, own_grad, returned).astype(single)
        seg_ids = segments(lax.dynamic_index_in_dim(lengths, micro_index, 0, False), positions)
        first_slot = min(max(moment - 1, 0), micro_count - 1)
        second_slot = min(moment, micro_count - 1) + 1
        saved = jax.tree.map(
            lambda early_leaf, late_leaf: jnp.where(is_first, early_leaf, late_leaf),
            kept_list[first_slot],
            kept_list[second_slot],
        )
        complete = saved
        grad_stream, updates = backward_pass(complete, grad_result, seg_ids, params)
        back_value = grad_stream.astype(bfloat)
        back_list.append(back_value)
        if moment < micro_count:
            returned = passed_along(back_value, "pipe", -1)
        totals = tuple(
            (running + jnp.where(active, update, 0.0) for running, update in zip(totals, updates))
        )
    forward_all = jnp.stack(sent_list)
    layer_out = jnp.where(section_id == 0, forward_all[:micro_count], forward_all[1:])
    backward_all = jnp.stack(back_list)
    input_grad = jnp.where(section_id == 1, backward_all[:micro_count], backward_all[1:])
    sum_norms, sum_qkv, sum_maps, sum_out, sum_up, sum_down = totals
    sum_pairs = sum_qkv[:, : 2 * D]
    sum_value = sum_qkv[:, 2 * D :]
    half_norms, half_pairs, half_value, half_maps, half_out, half_up, half_down = (
        lax.psum_scatter(sum_norms[None], "dp", scatter_dimension=2, tiled=True),
        lax.psum_scatter(sum_pairs[None], "dp", scatter_dimension=2, tiled=True),
        lax.psum_scatter(sum_value[None], "dp", scatter_dimension=2, tiled=True),
        lax.psum_scatter(sum_maps[None], "dp", scatter_dimension=2, tiled=True),
        lax.psum_scatter(sum_out[None], "dp", scatter_dimension=2, tiled=True),
        lax.psum_scatter(sum_up[None], "dp", scatter_dimension=2, tiled=True),
        lax.psum_scatter(sum_down[None], "dp", scatter_dimension=2, tiled=True),
    )
    reduced = (
        lax.psum_scatter(half_norms, "seq", scatter_dimension=2, tiled=True),
        lax.psum_scatter(half_pairs, "seq", scatter_dimension=2, tiled=True),
        lax.psum_scatter(half_value, "seq", scatter_dimension=2, tiled=True),
        lax.psum_scatter(half_maps, "seq", scatter_dimension=2, tiled=True),
        lax.psum_scatter(half_out, "seq", scatter_dimension=2, tiled=True),
        lax.psum_scatter(half_up, "seq", scatter_dimension=2, tiled=True),
        lax.psum_scatter(half_down, "seq", scatter_dimension=2, tiled=True),
    )
    return (
        layer_out[None],
        input_grad[None],
        reduced[0],
        reduced[1],
        reduced[2],
        reduced[3],
        reduced[4],
        reduced[5],
        reduced[6],
    )


FF = 3072
BLK = 256
THIN = D // 16
WIDE = FF // 16
REST_A = 2 * THIN
REST_B = 2 * THIN + 16
bfloat = jnp.bfloat16
single = jnp.float32
VMEM_BYTES = 60 * 1024 * 1024
HBM = pl.BlockSpec(memory_space=pl.ANY)
SMEM = pl.BlockSpec(memory_space=pltpu.SMEM)
VMEM = pl.BlockSpec(memory_space=pltpu.VMEM)


def dot_nn(a, b):
    return lax.dot_general(a, b, (((1,), (0,)), ((), ())), preferred_element_type=single)


def dot_nt(a, b):
    return lax.dot_general(a, b, (((1,), (1,)), ((), ())), preferred_element_type=single)


def dot_tn(a, b):
    return lax.dot_general(a, b, (((0,), (0,)), ((), ())), preferred_element_type=single)


def standardize(stream):
    centred = stream - jnp.mean(stream, -1, keepdims=True)
    scale = lax.rsqrt(jnp.mean(centred * centred, -1, keepdims=True) + 1e-05)
    return centred * scale, scale


def standardize_back(grad, unit, scale, gain):
    grad_unit = grad * gain
    return scale * (
        grad_unit
        - jnp.mean(grad_unit, -1, keepdims=True)
        - unit * jnp.mean(grad_unit * unit, -1, keepdims=True)
    )


def softmax_pair(logits):
    up = jnp.exp(logits - jnp.max(logits, 0, keepdims=True))
    down = jnp.exp(jnp.min(logits, 0, keepdims=True) - logits)
    up = up * (1.0 / jnp.sum(up, 0, keepdims=True))
    down = down * (1.0 / jnp.sum(down, 0, keepdims=True))
    return jnp.concatenate([up, down], 0).astype(bfloat)


def softmax_pair_back(feats, grad):
    up, down = feats[:HD].astype(single), feats[HD:].astype(single)
    grad_up, grad_down = grad[:HD], grad[HD:]
    grad_up = up * (grad_up - jnp.sum(up * grad_up, 0, keepdims=True))
    grad_down = down * (grad_down - jnp.sum(down * grad_down, 0, keepdims=True))
    return (grad_up - grad_down).astype(bfloat)


def fill_mask(info, mask_ref):
    rows = mask_ref.shape[0]
    source = lax.broadcasted_iota(jnp.int32, (rows, rows), 0)
    target = lax.broadcasted_iota(jnp.int32, (rows, rows), 1)
    allowed = source <= target
    for index in range(4):
        end = info[4 + index]
        allowed = allowed & ((source >= end) | (target < end))
    mask_ref[...] = jnp.where(allowed, 1.0, 0.0).astype(bfloat)


def block_maps(wfeat_ref, group):
    cols = wfeat_ref[:, pl.ds(group * BLK, BLK)]
    tall = jnp.concatenate([cols] * (BLK // HD), 0)
    row = lax.broadcasted_iota(jnp.int32, (BLK, BLK), 0) // HD
    col = lax.broadcasted_iota(jnp.int32, (BLK, BLK), 1) // HD
    return jnp.where(row == col, tall, jnp.zeros_like(tall))


def with_ones(values_t):
    count = values_t.shape[1]
    row = lax.broadcasted_iota(jnp.int32, (16, count), 0)
    extra = jnp.where(row < 2, 1.0, 0.0).astype(bfloat)
    return jnp.concatenate([values_t, extra], 0)


class Kept(NamedTuple):
    normed: Any
    qk: Any
    qft: Any
    kft: Any
    vt: Any
    ot: Any
    rden: Any
    mixed: Any
    middle: Any
    normed_two: Any
    hidden: Any
    slope: Any
    result: Any


KEPT = len(Kept._fields)


def kept_shapes(t):
    return Kept(
        normed=jax.ShapeDtypeStruct((t, D), bfloat),
        qk=jax.ShapeDtypeStruct((t, 2 * D), bfloat),
        qft=jax.ShapeDtypeStruct((2 * D, t), bfloat),
        kft=jax.ShapeDtypeStruct((2 * D, t), bfloat),
        vt=jax.ShapeDtypeStruct((D, t), bfloat),
        ot=jax.ShapeDtypeStruct((D, t), single),
        rden=jax.ShapeDtypeStruct((16, t), single),
        mixed=jax.ShapeDtypeStruct((t, D), bfloat),
        middle=jax.ShapeDtypeStruct((t, D), single),
        normed_two=jax.ShapeDtypeStruct((t, D), bfloat),
        hidden=jax.ShapeDtypeStruct((t, FF), bfloat),
        slope=jax.ShapeDtypeStruct((t, FF), bfloat),
        result=jax.ShapeDtypeStruct((t, D), bfloat),
    )


def scratch_like(shapes):
    return [pltpu.VMEM(shape.shape, shape.dtype) for shape in shapes]


def cost(micros):
    return pl.CostEstimate(flops=int(micros * 1e9), bytes_accessed=0, transcendentals=0)


def forward_kernel(core, aliased, *refs):
    info, x_ref, norm_ref, wfeat_ref, wqkv_h, wout_h, wup_h, wdown_h = refs[:8]
    refs = refs[8 + (KEPT if aliased else 0) :]
    outs, kept = Kept(*refs[:KEPT]), Kept(*refs[KEPT : 2 * KEPT])
    wqkv, wout, wup, wdown, mask, sem_in, sem_out = refs[2 * KEPT :]
    rows = x_ref.shape[0]

    def body():
        loads = [
            pltpu.make_async_copy(src, dst, sem_in.at[i])
            for i, (src, dst) in enumerate(
                ((wqkv_h, wqkv), (wout_h, wout), (wup_h, wup), (wdown_h, wdown))
            )
        ]
        for load in loads:
            load.start()
        stores = Kept(
            *[
                pltpu.make_async_copy(src, dst, sem_out.at[i])
                for i, (src, dst) in enumerate(zip(kept, outs))
            ]
        )
        unit, unused = standardize(x_ref[...].astype(single))
        kept.normed[...] = (unit * norm_ref[0:1] + norm_ref[1:2]).astype(bfloat)
        stores.normed.start()
        fill_mask(info, mask)
        loads[0].wait()
        normed = kept.normed[...]
        for group in range(6):
            part = dot_nn(normed, wqkv[:, group * BLK : (group + 1) * BLK]).astype(bfloat)
            kept.qk[:, group * BLK : (group + 1) * BLK] = part
            logits_t = dot_nn(part, block_maps(wfeat_ref, group)).T
            target = kept.qft if group < 3 else kept.kft
            for head in range(BLK // HD):
                start = ((group % 3) * (BLK // HD) + head) * 2 * HD
                target[start : start + 2 * HD, :] = softmax_pair(
                    logits_t[head * HD : (head + 1) * HD]
                )
        centres = []
        for group in range(3):
            part = dot_nn(normed, wqkv[:, 2 * D + group * BLK : 2 * D + (group + 1) * BLK])
            part_t = part.T
            centre = jnp.mean(part_t, 1, keepdims=True)
            centres.append(centre)
            kept.vt[group * BLK : (group + 1) * BLK, :] = (part_t - centre).astype(bfloat)
        for store in (stores.qk, stores.qft, stores.kft, stores.vt):
            store.start()
        kept.rden[...] = jnp.zeros_like(kept.rden)

        def head_step(head):
            wide = pl.ds(head * 2 * HD, 2 * HD)
            thin = pl.ds(head * HD, HD)
            keys = kept.kft[wide, :].T
            queries_t = kept.qft[wide, :]
            values_t = with_ones(kept.vt[thin, :])
            for block in range(rows // BLK):
                here = slice(block * BLK, (block + 1) * BLK)
                past = slice(0, (block + 1) * BLK)
                weights = dot_nn(keys[past], queries_t[:, here]).astype(bfloat) * mask[past, here]
                summed = dot_nn(values_t[:, past], weights)
                inverse = 1.0 / summed[HD : HD + 1]
                kept.rden[pl.ds(head, 1), here] = inverse
                kept.ot[thin, here] = summed[:HD] * inverse

        for head in range(H):
            head_step(head)

        stores.rden.start()
        stores.ot.start()
        for group in range(3):
            part = kept.ot[group * BLK : (group + 1) * BLK, :] + centres[group]
            kept.mixed[:, group * BLK : (group + 1) * BLK] = part.T.astype(bfloat)
        stores.mixed.start()
        loads[1].wait()
        kept.middle[...] = x_ref[...].astype(single) + dot_nn(kept.mixed[...], wout[...])
        stores.middle.start()
        unit, unused = standardize(kept.middle[...])
        kept.normed_two[...] = (unit * norm_ref[2:3] + norm_ref[3:4]).astype(bfloat)
        stores.normed_two.start()
        loads[2].wait()
        root = 0.7978845608028654
        for tile in range(FF // D):
            cols = slice(tile * D, (tile + 1) * D)
            pre = dot_nn(kept.normed_two[...], wup[:, cols])
            square = pre * pre
            bent = jnp.tanh(pre * (root + (root * 0.044715) * square))
            half = 0.5 + 0.5 * bent
            kept.hidden[:, cols] = (pre * half).astype(bfloat)
            slope = half + (pre * (half * (1.0 - bent))) * (root + (3 * root * 0.044715) * square)
            kept.slope[:, cols] = slope.astype(bfloat)
        stores.hidden.start()
        stores.slope.start()
        loads[3].wait()
        result = kept.middle[...] + dot_nn(kept.hidden[...], wdown[...])
        kept.result[...] = result.astype(bfloat)
        stores.result.start()
        for store in stores:
            store.wait()

    pl.when(info[0] == core)(body)


def forward_call(core, info, x, norm, wfeat, wqkv, wout, wup, wdown, previous=()):
    rows = x.shape[0]
    shapes = kept_shapes(rows)
    kept = pl.pallas_call(
        functools.partial(forward_kernel, core, bool(previous)),
        out_shape=list(shapes),
        in_specs=[SMEM, VMEM, VMEM, VMEM] + [HBM] * (4 + len(previous)),
        out_specs=[HBM] * KEPT,
        scratch_shapes=scratch_like(shapes)
        + scratch_like((wqkv, wout, wup, wdown))
        + [
            pltpu.VMEM((rows, rows), bfloat),
            pltpu.SemaphoreType.DMA((4,)),
            pltpu.SemaphoreType.DMA((KEPT,)),
        ],
        input_output_aliases={8 + i: i for i in range(len(previous))},
        compiler_params=pltpu.CompilerParams(vmem_limit_bytes=VMEM_BYTES),
        cost_estimate=cost(25),
        name="layer_forward",
    )(info, x, norm, wfeat, wqkv, wout, wup, wdown, *previous)
    return Kept(*kept)


def ship(info, stage, keep, send, first, sem, shards=range(16)):
    rows = keep.shape[2]
    copies = []
    for shard in shards:
        z, y, x = shard // 4, shard // 2 % 2, shard % 2
        own, index = (x, y) if first == 1 else (y, x)
        mine = own == info[first]
        source = stage.at[pl.ds(shard * rows, rows)]

        @pl.when(mine)
        def _():
            pltpu.make_async_copy(source, keep.at[z, index], sem).start()

        @pl.when(jnp.logical_not(mine))
        def _():
            pltpu.make_async_copy(source, send.at[z, index], sem).start()

        copies.append(pltpu.make_async_copy(source, keep.at[z, index], sem))
    return copies


def place(stage, part, at, rows, first_shard=0):
    size = stage.shape[0] // 16
    part = part.astype(bfloat)
    for index in range(part.shape[0] // rows):
        start = (first_shard + index) * size + at
        stage[start : start + rows, :] = part[index * rows : (index + 1) * rows]


def halves(*sizes):
    return [jax.ShapeDtypeStruct((4, 2, rows, D), bfloat) for rows in sizes for _ in range(2)]


def stages_of(*sizes):
    return [pltpu.VMEM((16 * rows, D), bfloat) for rows in sizes]


def ff_back_kernel(core, late, *refs):
    info, g_ref, norm_ref, hidden_h, wdown_h, wup_h, slope_h, normed_two_h, middle_h = refs[:9]
    refs = refs[9 + late :]
    g_middle_o, gnorm_o, keep_a, send_a, keep_b, send_b = refs[:6]
    hidden, wdown, wup, slope, normed_two, middle, g_pre, g_middle = refs[6:14]
    stage_a, stage_b, sem_in, sem_out = refs[14:]

    def body():
        sources = (hidden_h, wdown_h, slope_h, normed_two_h, wup_h, middle_h)
        targets = (hidden, wdown, slope, normed_two, wup, middle)
        loads = [
            pltpu.make_async_copy(src, dst, sem_in.at[i])
            for i, (src, dst) in enumerate(zip(sources, targets))
        ]
        for load in loads:
            load.start()
        g = g_ref[...]
        g_t = g.T
        loads[0].wait()
        for tile in range(FF // D):
            place(stage_a, dot_nn(g_t, hidden[:, tile * D : (tile + 1) * D]), tile * THIN, THIN)
        copies = ship(info, stage_a, keep_a, send_a, 1, sem_out.at[0])
        for load in loads[1:4]:
            load.wait()
        for tile in range(FF // D):
            cols = slice(tile * D, (tile + 1) * D)
            g_hidden = dot_nt(g, wdown[cols, :])
            g_pre[:, cols] = (g_hidden * slope[:, cols].astype(single)).astype(bfloat)
            place(stage_b, dot_tn(g_pre[:, cols], normed_two[...]), 0, WIDE, 4 * tile)
            shards = range(4 * tile, 4 * tile + 4)
            copies += ship(info, stage_b, keep_b, send_b, 2, sem_out.at[1], shards)
        loads[4].wait()
        g_normed = dot_nt(g_pre[...], wup[...])
        loads[5].wait()
        unit, scale = standardize(middle[...])
        gnorm_o[0:1, :] = jnp.sum(g_normed * unit, 0, keepdims=True)
        gnorm_o[1:2, :] = jnp.sum(g_normed, 0, keepdims=True)
        g_middle[...] = g.astype(single) + standardize_back(g_normed, unit, scale, norm_ref[2:3])
        copies.append(pltpu.make_async_copy(g_middle, g_middle_o, sem_out.at[2]))
        copies[-1].start()
        for copy in copies:
            copy.wait()

    pl.when(info[0] == core)(body)


def ff_back_call(core, info, g, norm, wdown, wup, kept, after):
    rows = g.shape[0]
    shapes = [
        jax.ShapeDtypeStruct((rows, D), single),
        jax.ShapeDtypeStruct((2, D), single),
    ]
    loads = (kept.hidden, wdown, wup, kept.slope, kept.normed_two, kept.middle)
    return pl.pallas_call(
        functools.partial(ff_back_kernel, core, len(after)),
        out_shape=shapes + halves(WIDE, WIDE),
        in_specs=[SMEM, VMEM, VMEM] + [HBM] * (6 + len(after)),
        out_specs=[HBM, VMEM] + [HBM] * 4,
        scratch_shapes=scratch_like(loads)
        + [pltpu.VMEM((rows, FF), bfloat), pltpu.VMEM((rows, D), single)]
        + stages_of(WIDE, WIDE)
        + [pltpu.SemaphoreType.DMA((6,)), pltpu.SemaphoreType.DMA((3,))],
        compiler_params=pltpu.CompilerParams(vmem_limit_bytes=VMEM_BYTES),
        cost_estimate=cost(18),
        name="feed_forward_backward",
    )(info, g, norm, *loads, *after)


def mix_loads(kept):
    return kept.mixed, kept.qft, kept.kft, kept.vt, kept.ot, kept.rden, kept.qk, kept.normed


def mix_back_kernel(core, aliased, *refs):
    info, g_middle_ref, x_ref, norm_ref, gnorm_two_ref, wfeat_ref, wout_h, wqkv_h = refs[:8]
    kept_h = refs[8:16]
    refs = refs[16 + (1 if aliased else 0) :]
    g_stream_o, keep_a, send_a, keep_b, send_b = refs[:5]
    mixed, qft, kft, vt, ot, rden, qk, normed = refs[5:13]
    wout, wqkv, mask, gm_t, gl_t, gv_t, joined, misc, g_stream = refs[13:22]
    stage_a, stage_b, sem_in, sem_out = refs[22:]
    rows = x_ref.shape[0]

    def body():
        sources = (wout_h,) + tuple(kept_h) + (wqkv_h,)
        targets = (wout, mixed, qft, kft, vt, ot, rden, qk, normed, wqkv)
        loads = [
            pltpu.make_async_copy(src, dst, sem_in.at[i])
            for i, (src, dst) in enumerate(zip(sources, targets))
        ]
        for load in loads:
            load.start()
        branch = g_middle_ref[...].astype(bfloat)
        fill_mask(info, mask)
        loads[0].wait()
        gm_t[...] = dot_nt(wout[...], branch)
        loads[1].wait()
        place(stage_a, dot_tn(branch, mixed[...]), 0, THIN)
        for load in loads[2:7]:
            load.wait()

        def head_step(head):
            wide = pl.ds(head * 2 * HD, 2 * HD)
            thin = pl.ds(head * HD, HD)
            keys_t, queries_t = kft[wide, :], qft[wide, :]
            keys = keys_t.T
            values = with_ones(vt[thin, :]).T
            inverse = rden[pl.ds(head, 1), :]
            grad = gm_t[thin, :]
            tilt = -jnp.sum(grad * ot[thin, :], 0, keepdims=True) * inverse
            high = tilt.astype(bfloat).astype(single)
            grad = grad * inverse
            fill = jnp.zeros((14, rows), single)
            grads_t = jnp.concatenate([grad, high, tilt - high, fill], 0).astype(bfloat)
            grad_low = grads_t[:HD]
            g_query = []
            g_key = [None] * (rows // BLK)
            g_value = [None] * (rows // BLK)
            for block in range(rows // BLK):
                here = slice(block * BLK, (block + 1) * BLK)
                past = slice(0, (block + 1) * BLK)
                allowed = mask[past, here]
                weights = dot_nn(keys[past], queries_t[:, here]).astype(bfloat) * allowed
                g_weights = dot_nn(values[past], grads_t[:, here]).astype(bfloat) * allowed
                g_query.append(dot_nn(keys_t[:, past], g_weights))
                for other in range(block + 1):
                    part = slice(other * BLK, (other + 1) * BLK)
                    more_key = dot_nt(queries_t[:, here], g_weights[part])
                    more_value = dot_nt(grad_low[:, here], weights[part])
                    g_key[other] = more_key if g_key[other] is None else g_key[other] + more_key
                    g_value[other] = (
                        more_value if g_value[other] is None else g_value[other] + more_value
                    )
            gl_t[thin, :] = softmax_pair_back(queries_t, jnp.concatenate(g_query, 1))
            later = pl.ds(D + head * HD, HD)
            gl_t[later, :] = softmax_pair_back(keys_t, jnp.concatenate(g_key, 1))
            gv_t[thin, :] = jnp.concatenate(g_value, 1).astype(bfloat)

        for head in range(H):
            head_step(head)

        loads[7].wait()
        for group in range(6):
            span = slice(group * BLK, (group + 1) * BLK)
            part_t = gl_t[span, :]
            joined[:, span] = dot_nt(part_t.T, block_maps(wfeat_ref, group)).astype(bfloat)
            cross = dot_nn(part_t, qk[:, span])
            for head in range(BLK // HD):
                first = group * BLK + head * HD
                misc[first : first + HD, 0:HD] = cross[
                    head * HD : (head + 1) * HD, head * HD : (head + 1) * HD
                ].astype(bfloat)
        for group in range(3):
            span = slice(group * BLK, (group + 1) * BLK)
            joined[:, 2 * D + group * BLK : 2 * D + (group + 1) * BLK] = gv_t[span, :].T
        loads[8].wait()
        base = normed[...]
        place(stage_a, dot_nn(gv_t[...], base), THIN, THIN)
        copies = ship(info, stage_a, keep_a, send_a, 1, sem_out.at[0])
        for group in range(2):
            part = dot_tn(joined[:, group * D : (group + 1) * D], base)
            place(stage_b, part, 0, 2 * THIN, 8 * group)
        loads[9].wait()
        g_normed = dot_nt(joined[...], wqkv[...])
        unit, scale = standardize(x_ref[...].astype(single))
        norm_rows = jnp.concatenate(
            [
                jnp.sum(g_normed * unit, 0, keepdims=True),
                jnp.sum(g_normed, 0, keepdims=True),
                gnorm_two_ref[...],
                jnp.zeros((124, D), single),
            ],
            0,
        )
        turned = norm_rows.T.astype(bfloat)
        for shard in range(16):
            start = (shard + 1) * REST_B - 16
            for block in range(6):
                source = shard * 2 * THIN + block * 16
                lanes = slice(block * 2 * HD, block * 2 * HD + HD)
                stage_b[start : start + 16, lanes] = misc[source : source + 16, :HD]
                source = shard * THIN + min(block, 2) * 16
                lanes = slice(block * 2 * HD + HD, (block + 1) * 2 * HD)
                stage_b[start : start + 16, lanes] = turned[source : source + 16, :HD]
        copies += ship(info, stage_b, keep_b, send_b, 2, sem_out.at[1])
        total = g_middle_ref[...] + standardize_back(g_normed, unit, scale, norm_ref[0:1])
        g_stream[...] = total.astype(bfloat)
        copies.append(pltpu.make_async_copy(g_stream, g_stream_o, sem_out.at[2]))
        copies[-1].start()
        for copy in copies:
            copy.wait()

    pl.when(info[0] == core)(body)


def mix_back_call(core, info, g_middle, x, norm, gnorm_two, wfeat, wout, wqkv, kept, previous):
    rows = x.shape[0]
    shapes = [jax.ShapeDtypeStruct((rows, D), bfloat)] + halves(REST_A, REST_B)
    return pl.pallas_call(
        functools.partial(mix_back_kernel, core, bool(previous)),
        out_shape=shapes,
        in_specs=[SMEM] + [VMEM] * 5 + [HBM] * (10 + len(previous)),
        out_specs=[HBM] * 5,
        scratch_shapes=scratch_like(mix_loads(kept) + (wout, wqkv))
        + [
            pltpu.VMEM((rows, rows), bfloat),
            pltpu.VMEM((D, rows), single),
            pltpu.VMEM((2 * D, rows), bfloat),
            pltpu.VMEM((D, rows), bfloat),
            pltpu.VMEM((rows, 3 * D), bfloat),
            pltpu.VMEM((2 * D, 2 * HD), bfloat),
            pltpu.VMEM((rows, D), bfloat),
        ]
        + stages_of(REST_A, REST_B)
        + [pltpu.SemaphoreType.DMA((10,)), pltpu.SemaphoreType.DMA((3,))],
        input_output_aliases={16: 0} if previous else {},
        compiler_params=pltpu.CompilerParams(vmem_limit_bytes=VMEM_BYTES),
        cost_estimate=cost(22),
        name="mix_backward",
    )(
        info,
        g_middle,
        x,
        norm,
        gnorm_two,
        wfeat,
        wout,
        wqkv,
        *mix_loads(kept),
        *previous,
    )


class Travel(NamedTuple):
    keep_a: Any
    keep_b: Any
    one_a: Any
    one_b: Any
    two_a: Any = None
    two_b: Any = None
    low: Any = None
    high: Any = None


def at_shard(travel, rows_a, z, x, y, z_high):
    span_a, span_b = pl.ds(0, rows_a), pl.ds(rows_a, travel.keep_b.shape[2])
    terms = [
        ((travel.keep_a.at[z, y], span_a), (travel.keep_b.at[z, x], span_b)),
        ((travel.one_a.at[z, y], span_a), (travel.one_b.at[z, x], span_b)),
    ]
    if travel.two_a is not None:
        terms.append(((travel.two_a.at[z], span_a), (travel.two_b.at[z], span_b)))
    if travel.low is not None:
        terms.append(((travel.low.at[z_high], pl.ds(0, rows_a + travel.keep_b.shape[2])),))
    if travel.high is not None:
        terms.append(((travel.high, pl.ds(0, rows_a + travel.keep_b.shape[2])),))
    return terms


def fetch(terms, held, sems):
    copies = []
    for index, pieces in enumerate(terms):
        for piece, (source, span) in enumerate(pieces):
            copies.append(
                pltpu.make_async_copy(source, held.at[index, span], sems.at[index, piece])
            )
    for copy in copies:
        copy.start()
    return copies


def total_of(held, count):
    total = held[0].astype(single)
    for index in range(1, count):
        total = total + held[index].astype(single)
    return total


def second_hop_kernel(core, info, keep_a, keep_b, one_a, one_b, after, out_a, out_b, *scratch):
    held_a, more_a, held_b, more_b, sem_in, sem_out = scratch

    def body():
        x, y = info[1], info[2]
        plan = (
            (keep_a.at[:, 1 - y], one_a.at[:, 1 - y], held_a, more_a, out_a),
            (keep_b.at[:, 1 - x], one_b.at[:, 1 - x], held_b, more_b, out_b),
        )
        copies = []
        for index, (keep, came, held, more, unused) in enumerate(plan):
            copies.append(pltpu.make_async_copy(keep, held, sem_in.at[2 * index]))
            copies.append(pltpu.make_async_copy(came, more, sem_in.at[2 * index + 1]))
        for copy in copies:
            copy.start()
        stores = []
        for index, (unused, unused, held, more, out) in enumerate(plan):
            copies[2 * index].wait()
            copies[2 * index + 1].wait()
            held[...] = (held[...].astype(single) + more[...].astype(single)).astype(bfloat)
            stores.append(pltpu.make_async_copy(held, out, sem_out.at[index]))
            stores[-1].start()
        for store in stores:
            store.wait()

    pl.when(info[0] == core)(body)


def second_hop_call(core, info, travel, after):
    shapes = [
        jax.ShapeDtypeStruct((4,) + keep.shape[2:], bfloat)
        for keep in (travel.keep_a, travel.keep_b)
    ]
    return pl.pallas_call(
        functools.partial(second_hop_kernel, core),
        out_shape=shapes,
        in_specs=[SMEM] + [HBM] * 5,
        out_specs=[HBM] * 2,
        scratch_shapes=scratch_like((shapes[0], shapes[0], shapes[1], shapes[1]))
        + [pltpu.SemaphoreType.DMA((4,)), pltpu.SemaphoreType.DMA((2,))],
        compiler_params=pltpu.CompilerParams(vmem_limit_bytes=VMEM_BYTES),
        cost_estimate=cost(3),
        name="for_second_hop",
    )(info, travel.keep_a, travel.keep_b, travel.one_a, travel.one_b, after)


def z_hop_kernel(core, count, info, *refs):
    travel, refs = Travel(*refs[:count]), refs[count + 1 :]
    out, held, total, sem_in, sem_out = refs
    rows_a = travel.keep_a.shape[2]

    def body():
        x, y, z = info[1], info[2], info[3]
        low, high = z % 2, z // 2
        if travel.low is None:
            targets = [((1 - low), 0), (2 + (1 - low), 1)]
        else:
            targets = [(2 * (1 - high) + low, 1 - high)]
        copies = [
            fetch(
                at_shard(travel, rows_a, target, x, y, target_high),
                held.at[index],
                sem_in.at[index],
            )
            for index, (target, target_high) in enumerate(targets)
        ]
        stores = []
        for index in range(len(targets)):
            for copy in copies[index]:
                copy.wait()
            count_terms = 3 if travel.low is None else 4
            total[index] = total_of(held.at[index], count_terms).astype(bfloat)
            to = out.at[index] if travel.low is None else out
            stores.append(pltpu.make_async_copy(total.at[index], to, sem_out.at[index]))
            stores[-1].start()
        for store in stores:
            store.wait()

    pl.when(info[0] == core)(body)


def z_hop_call(core, info, travel, after):
    rows = travel.keep_a.shape[2] + travel.keep_b.shape[2]
    refs = [ref for ref in travel if ref is not None]
    shape = (2, rows, D) if travel.low is None else (rows, D)
    return pl.pallas_call(
        functools.partial(z_hop_kernel, core, len(refs)),
        out_shape=jax.ShapeDtypeStruct(shape, bfloat),
        in_specs=[SMEM] + [HBM] * (len(refs) + 1),
        out_specs=HBM,
        scratch_shapes=[
            pltpu.VMEM((2, 4, rows, D), bfloat),
            pltpu.VMEM((2, rows, D), bfloat),
            pltpu.SemaphoreType.DMA((2, 4, 2)),
            pltpu.SemaphoreType.DMA((2,)),
        ],
        compiler_params=pltpu.CompilerParams(vmem_limit_bytes=VMEM_BYTES),
        cost_estimate=cost(2),
        name="for_z_hop",
    )(info, *refs, after)


def finish_kernel(write, info, *refs):
    travels = Travel(*refs[:8]), Travel(*refs[8:16])
    outs = refs[16:-2]
    held, sem_in = refs[-2:]

    def bring(travel):
        x, y, z = info[1], info[2], info[3]
        rows_a = travel.keep_a.shape[2]
        for copy in fetch(at_shard(travel, rows_a, z, x, y, z // 2), held, sem_in):
            copy.wait()

    for core in range(2):
        pl.when(info[0] == core)(functools.partial(bring, travels[core]))
    write(total_of(held, 5), outs)


def write_early(total, outs):
    down, up = outs
    for tile in range(FF // D):
        down[0, :, tile * D : (tile + 1) * D] = total[tile * THIN : (tile + 1) * THIN]
    up[0] = total[WIDE:]


def write_rest(total, outs):
    norms, pairs, value, maps, out = outs
    out[0] = total[:THIN]
    value[0] = total[THIN : 2 * THIN]
    pairs[0] = total[2 * THIN : 4 * THIN]
    misc = total[4 * THIN :]
    tall = [misc[:, i * 2 * HD : (i + 1) * 2 * HD] for i in range(6)]
    wide = jnp.concatenate(tall + [jnp.zeros((32, 2 * HD), single)], 0).T
    maps[0] = wide[:HD, : 2 * THIN]
    norms[0] = wide[HD : HD + 4, :THIN]


def finish_call(info, first, second, shapes, write):
    rows = first.keep_a.shape[2] + first.keep_b.shape[2]
    return pl.pallas_call(
        functools.partial(finish_kernel, write),
        out_shape=[jax.ShapeDtypeStruct((1,) + shape, single) for shape in shapes],
        in_specs=[SMEM] + [HBM] * 16,
        out_specs=[VMEM] * len(shapes),
        scratch_shapes=[
            pltpu.VMEM((5, rows, D), bfloat),
            pltpu.SemaphoreType.DMA((5, 2)),
        ],
        compiler_params=pltpu.CompilerParams(vmem_limit_bytes=VMEM_BYTES),
        cost_estimate=cost(3),
        name="shard_gradients",
    )(info, *first, *second)


def swap_on(value, core, axis, bit):
    count = lax.axis_size(axis)
    pairs = [(core * count + i, core * count + (i ^ bit)) for i in range(count)]
    return lax.ppermute(value, ("pipe", axis), pairs)


def fast_on_device(
    tokens,
    cotangent,
    lengths,
    norm_params,
    qkv_weight,
    feature_weight,
    out_weight,
    up_weight,
    down_weight,
):
    norm, wqkv, wfeat = norm_params[0], qkv_weight[0], feature_weight[0]
    wout, wup, wdown = out_weight[0], up_weight[0], down_weight[0]
    pipe, seq = lax.axis_index("pipe"), lax.axis_index("seq")
    ends = jnp.cumsum(lax.dynamic_index_in_dim(lengths, seq, 0, False)).astype(jnp.int32)
    places = jnp.stack([pipe, seq % 2, seq // 2, lax.axis_index("dp")]).astype(jnp.int32)
    info = jnp.concatenate([places, ends])
    mine = jnp.where(pipe == 0, tokens, cotangent)
    whole = lax.all_to_all(mine, "seq", 0, 0, tiled=True).reshape(-1, D)

    def one(core, parts):
        keep_a, send_a, keep_b, send_b = parts
        return Travel(
            keep_a, keep_b, swap_on(send_a, core, "seq", 1), swap_on(send_b, core, "seq", 2)
        )

    def two(core, travel, after):
        send_a, send_b = second_hop_call(core, info, travel, after)
        return send_a, travel._replace(
            two_a=swap_on(send_a, core, "seq", 2), two_b=swap_on(send_b, core, "seq", 1)
        )

    def low(core, travel, after):
        send = z_hop_call(core, info, travel, after)
        return send, travel._replace(low=swap_on(send, core, "dp", 1))

    def high(core, travel, after):
        send = z_hop_call(core, info, travel, after)
        return send, travel._replace(high=swap_on(send, core, "dp", 2))

    def ff_back(core, grad, after=()):
        return ff_back_call(core, info, grad, norm, wdown, wup, kept, after)

    def mix_back(core, x, g_middle, gnorm_two, previous=()):
        return mix_back_call(
            core, info, g_middle, x, norm, gnorm_two, wfeat, wout, wqkv, kept, previous
        )

    kept = forward_call(0, info, whole, norm, wfeat, wqkv, wout, wup, wdown)
    sent = lax.ppermute(kept.result, "pipe", [(0, 1)])
    kept = forward_call(1, info, sent, norm, wfeat, wqkv, wout, wup, wdown, kept)

    g_middle, gnorm_two, *parts = ff_back(1, whole)
    early_one = one(1, parts)
    g_stream, *parts = mix_back(1, sent, g_middle, gnorm_two)
    rest_one = one(1, parts)
    returned = lax.ppermute(g_stream, "pipe", [(1, 0)])

    last, early_one = two(1, early_one, g_stream)
    last, rest_one = two(1, rest_one, last)
    g_middle, gnorm_two, *parts = ff_back(0, returned, (last,))
    early_two = one(0, parts)
    g_stream, *parts = mix_back(0, whole, g_middle, gnorm_two, (g_stream,))
    rest_two = one(0, parts)
    last, early_two = two(0, early_two, g_stream)
    last, rest_two = two(0, rest_two, last)
    last, early_one = low(1, early_one, last)
    last, rest_one = low(1, rest_one, last)
    last, early_two = low(0, early_two, last)
    last, early_one = high(1, early_one, last)
    last, rest_two = low(0, rest_two, last)
    last, rest_one = high(1, rest_one, last)
    last, early_two = high(0, early_two, last)
    last, rest_two = high(0, rest_two, last)
    down, up = finish_call(info, early_two, early_one, [(THIN, FF), (WIDE, D)], write_early)
    norms, pairs, value, maps, out = finish_call(
        info,
        rest_two,
        rest_one,
        [(4, THIN), (2 * THIN, D), (THIN, D), (HD, 2 * THIN), (THIN, D)],
        write_rest,
    )
    down, up, pairs, value, out = [g.swapaxes(1, 2) for g in (down, up, pairs, value, out)]

    def back_to_rows(value):
        return lax.all_to_all(value.reshape(tokens.shape), "seq", 0, 0, tiled=True)[None]

    layer_out, input_grad = back_to_rows(kept.result), back_to_rows(g_stream)
    return layer_out, input_grad, norms, pairs, value, maps, out, up, down


def on_device(tokens, cotangent, lengths, *params):
    suits = (lax.axis_size("dp"), lax.axis_size("seq"), tokens.shape[0]) == (4, 4, 4)
    plan = fast_on_device if suits else general_on_device
    return plan(tokens, cotangent, lengths, *params)


def solution(mesh):
    in_specs = (
        P("dp", "seq", None),
        P("dp", "seq", None),
        P("dp", None),
        P("pipe", None, None),
        P("pipe", None, None),
        P("pipe", None, None),
        P("pipe", None, None),
        P("pipe", None, None),
        P("pipe", None, None),
    )
    out_specs = (
        P("pipe", "dp", "seq", None),
        P("pipe", "dp", "seq", None),
        P("pipe", None, ("dp", "seq")),
        P("pipe", None, ("dp", "seq")),
        P("pipe", None, ("dp", "seq")),
        P("pipe", None, ("dp", "seq")),
        P("pipe", None, ("dp", "seq")),
        P("pipe", None, ("dp", "seq")),
        P("pipe", None, ("dp", "seq")),
    )
    return jax.shard_map(
        on_device, mesh=mesh, in_specs=in_specs, out_specs=out_specs, check_vma=False
    )
```

```python
import functools
from typing import Any, NamedTuple

import jax
import jax.numpy as jnp
from jax import lax
from jax.experimental import pallas as pl
from jax.experimental.pallas import tpu as pltpu
from jax.sharding import PartitionSpec as P

D = 768
H = 12
HD = 64
CH = 64


highest = lax.Precision.HIGHEST
bfloat = jnp.bfloat16
single = jnp.float32


def carried_in_2(value, axis, join, neutral, backward):
    count, mine = (lax.axis_size(axis), lax.axis_index(axis))
    pieces = jax.tree.map(lambda part: lax.all_gather(part, axis), value)
    if backward:
        pieces = jax.tree.map(lambda part: part[::-1], pieces)
        mine = count - 1 - mine
    total = jax.tree.map(
        lambda part, zero: jnp.full_like(part, 0) + jnp.asarray(zero, part.dtype), value, neutral
    )

    def lap(position, total):
        longer = join(total, jax.tree.map(lambda part: part[position], pieces))
        return jax.tree.map(lambda new, old: jnp.where(position < mine, new, old), longer, total)

    return lax.fori_loop(0, count - 1, lap, total)


def for_sending(shard):
    return jax.tree.map(lambda a: a.astype(jnp.bfloat16) if a.dtype == jnp.float32 else a, shard)


def passed_along(shard, axis, by):
    length = lax.axis_size(axis)
    pairs = [(i, i + by) for i in range(length) if 0 <= i + by < length]
    return lax.ppermute(shard, axis, pairs)


def normalize(stream, norm_gain, norm_shift):
    centred = stream - jnp.mean(stream, -1, keepdims=True)
    spread = jnp.mean(centred * centred, -1, keepdims=True)
    return centred * lax.rsqrt(spread + 1e-05) * norm_gain + norm_shift


def features(logits):
    return jnp.concatenate([jax.nn.softmax(logits, -1), jax.nn.softmax(-logits, -1)], -1)


def flat_features(flat_logits):
    row_count = flat_logits.shape[0]
    return features(flat_logits.reshape(row_count, H, HD)).reshape(row_count, 2 * D)


def smooth(hidden_pre):
    return jax.nn.gelu(hidden_pre, approximate=True)


def segments(lengths_row, positions):
    doc_ends = jnp.cumsum(lengths_row)
    return jnp.sum((doc_ends[None, :] <= positions[:, None]).astype(jnp.int32), 1)


def span_step(carried_in, block_in):
    kv_state, norm_state, last_seg = carried_in
    query_feats, key_feats, values, seg_ids = block_in
    seg_float = seg_ids.astype(single)
    scores = jnp.einsum("thf,shf->hts", query_feats, key_feats, precision=highest)
    places = jnp.arange(CH, dtype=jnp.int32)
    allowed = (places[:, None] >= places[None, :]) & (seg_ids[:, None] == seg_ids[None, :])
    weights = jnp.where(allowed[None], scores, 0.0)
    carried = (seg_float == last_seg).astype(single)
    numerator = jnp.einsum("hts,shd->thd", weights, values, precision=highest) + carried[
        :, None, None
    ] * jnp.einsum("thf,hfd->thd", query_feats, kv_state, precision=highest)
    denominator = jnp.sum(weights, -1).T + carried[:, None] * jnp.einsum(
        "thf,hf->th", query_feats, norm_state, precision=highest
    )
    tail_seg = seg_float[-1]
    inside = (seg_float == tail_seg).astype(single)
    kept_part = (last_seg == tail_seg).astype(single)
    tail_keys = key_feats * inside[:, None, None]
    kv_state = kept_part * kv_state + jnp.einsum(
        "shf,shd->hfd", tail_keys, values, precision=highest
    )
    norm_state = kept_part * norm_state + jnp.sum(tail_keys, 0)
    return ((kv_state, norm_state, tail_seg), numerator / denominator[:, :, None])


def attend(query_feats, key_feats, values, seg_ids, kv_state, norm_state, last_seg):
    row_count = query_feats.shape[0]
    block_count = row_count // CH
    blocks = (
        query_feats.reshape(block_count, CH, H, 2 * HD),
        key_feats.reshape(block_count, CH, H, 2 * HD),
        values.reshape(block_count, CH, H, HD),
        seg_ids.reshape(block_count, CH),
    )
    closing, mixed_out = lax.scan(span_step, (kv_state, norm_state, last_seg), blocks)
    return mixed_out.reshape(row_count, H, HD)


def tail_state(key_feats, values, seg_ids):
    row_count = key_feats.shape[0]
    key_three = key_feats.reshape(row_count, H, 2 * HD)
    value_three = values.reshape(row_count, H, HD)
    seg_float = seg_ids.astype(single)
    tail_seg = seg_float[-1]
    tail_keys = key_three * (seg_float == tail_seg).astype(single)[:, None, None]
    return (
        jnp.einsum("shf,shd->hfd", tail_keys, value_three, precision=highest),
        jnp.sum(tail_keys, 0),
        tail_seg,
    )


def join_states(earlier, later):
    early_kv, early_norm, early_seg = earlier
    late_kv, late_norm, late_seg = later
    is_blank = late_seg < 0.0
    matches = early_seg == late_seg
    kv_sum = jnp.where(is_blank, early_kv, late_kv + jnp.where(matches, early_kv, 0.0))
    norm_sum = jnp.where(is_blank, early_norm, late_norm + jnp.where(matches, early_norm, 0.0))
    return (kv_sum, norm_sum, jnp.where(is_blank, early_seg, late_seg))


def empty_state():
    return (jnp.zeros((H, 2 * HD, HD), single), jnp.zeros((H, 2 * HD), single), jnp.float32(-1.0))


class Front(NamedTuple):
    stream: Any
    normed: Any
    queries: Any
    key_rows: Any
    values: Any
    q_logit: Any
    k_logit: Any
    query_feats: Any
    key_feats: Any


class Complete(NamedTuple):
    stream: Any
    normed: Any
    queries: Any
    key_rows: Any
    values: Any
    q_logit: Any
    k_logit: Any
    query_feats: Any
    key_feats: Any
    incoming_kv: Any
    incoming_norm: Any
    incoming_seg: Any
    mixed_low: Any
    middle: Any
    normed_two: Any
    hidden_pre: Any
    hidden: Any
    result: Any


def front_pass(section_input, params):
    norm_rows, w_qkv, w_feat = (params[0], params[1], params[2])
    stream = section_input.astype(single)
    row_count = stream.shape[0]
    normed = normalize(stream, norm_rows[0], norm_rows[1]).astype(bfloat)
    joined = jnp.dot(normed, w_qkv, preferred_element_type=single)
    queries = joined[:, :D].astype(bfloat)
    key_rows = joined[:, D : 2 * D].astype(bfloat)
    values = joined[:, 2 * D :]
    feat_maps = w_feat.reshape(HD, 2, H, HD)
    q_logit = jnp.einsum(
        "shd,dhe->she",
        queries.reshape(row_count, H, HD),
        feat_maps[:, 0],
        preferred_element_type=single,
    ).reshape(row_count, D)
    k_logit = jnp.einsum(
        "shd,dhe->she",
        key_rows.reshape(row_count, H, HD),
        feat_maps[:, 1],
        preferred_element_type=single,
    ).reshape(row_count, D)
    return Front(
        stream=stream,
        normed=normed,
        queries=queries,
        key_rows=key_rows,
        values=values,
        q_logit=q_logit,
        k_logit=k_logit,
        query_feats=flat_features(q_logit),
        key_feats=flat_features(k_logit),
    )


def rear_pass(front, incoming, seg_ids, params):
    norm_rows, w_out, w_up, w_down = (params[0], params[3], params[4], params[5])
    stream = front.stream
    row_count = stream.shape[0]
    mixed_out = attend(
        front.query_feats,
        front.key_feats,
        front.values,
        seg_ids,
        incoming[0],
        incoming[1],
        incoming[2],
    )
    mixed_low = mixed_out.reshape(row_count, D).astype(bfloat)
    middle = stream + jnp.dot(mixed_low, w_out, preferred_element_type=single)
    normed_two = normalize(middle, norm_rows[2], norm_rows[3]).astype(bfloat)
    hidden_pre = jnp.dot(normed_two, w_up, preferred_element_type=single)
    hidden = smooth(hidden_pre).astype(bfloat)
    result = middle + jnp.dot(hidden, w_down, preferred_element_type=single)
    return Complete(
        *front,
        incoming_kv=incoming[0],
        incoming_norm=incoming[1],
        incoming_seg=incoming[2],
        mixed_low=mixed_low,
        middle=middle,
        normed_two=normed_two,
        hidden_pre=hidden_pre,
        hidden=hidden,
        result=result,
    )


def backward_pass(complete, grad_result, seg_ids, params):
    norm_rows, w_qkv, w_feat, w_out, w_up, w_down = params
    row_count = grad_result.shape[0]
    down_grad = grad_result.astype(bfloat)
    grad_down = jnp.einsum(
        "sf,sd->fd", complete.hidden, down_grad, preferred_element_type=single
    )
    grad_hidden = jnp.einsum("sd,fd->sf", down_grad, w_down, preferred_element_type=single)
    unused, smooth_back = jax.vjp(smooth, complete.hidden_pre)
    pre_grad = smooth_back(grad_hidden)[0].astype(bfloat)
    grad_up = jnp.einsum(
        "sd,sf->df", complete.normed_two, pre_grad, preferred_element_type=single
    )
    grad_normed_two = jnp.einsum("sf,df->sd", pre_grad, w_up, preferred_element_type=single)
    unused, norm_back_two = jax.vjp(normalize, complete.middle, norm_rows[2], norm_rows[3])
    grad_middle, grad_gain_two, grad_shift_two = norm_back_two(grad_normed_two)
    grad_middle = grad_middle + grad_result
    branch_grad = grad_middle.astype(bfloat)
    grad_out = jnp.einsum(
        "sa,sd->ad", complete.mixed_low, branch_grad, preferred_element_type=single
    )
    grad_mixed = jnp.einsum("sd,ad->sa", branch_grad, w_out, preferred_element_type=single).reshape(
        row_count, H, HD
    )
    last_seg = complete.incoming_seg

    def core_attend(query_feats, key_feats, values, kv_state, norm_state):
        return attend(query_feats, key_feats, values, seg_ids, kv_state, norm_state, last_seg)

    unused, core_back = jax.vjp(
        core_attend,
        complete.query_feats,
        complete.key_feats,
        complete.values,
        complete.incoming_kv,
        complete.incoming_norm,
    )
    grad_qf, grad_kf, grad_values, grad_kv, grad_norm = core_back(grad_mixed)
    passed = carried_in_2((grad_kv, grad_norm, last_seg), "seq", join_states, empty_state(), True)

    def summary(key_feats, values):
        kv_sum, norm_sum, tail_seg = tail_state(key_feats, values, seg_ids)
        return (kv_sum, norm_sum)

    unused, summary_back = jax.vjp(summary, complete.key_feats, complete.values)
    extra_kf, extra_values = summary_back((passed[0], passed[1]))
    grad_kf = grad_kf + extra_kf
    grad_values = grad_values + extra_values
    unused, feat_back_q = jax.vjp(flat_features, complete.q_logit)
    unused, feat_back_k = jax.vjp(flat_features, complete.k_logit)
    q_logit_grad = feat_back_q(grad_qf)[0].astype(bfloat).reshape(row_count, H, HD)
    k_logit_grad = feat_back_k(grad_kf)[0].astype(bfloat).reshape(row_count, H, HD)
    feat_maps = w_feat.reshape(HD, 2, H, HD)
    grad_map_q = jnp.einsum(
        "shd,she->dhe",
        complete.queries.reshape(row_count, H, HD),
        q_logit_grad,
        preferred_element_type=single,
    )
    grad_map_k = jnp.einsum(
        "shd,she->dhe",
        complete.key_rows.reshape(row_count, H, HD),
        k_logit_grad,
        preferred_element_type=single,
    )
    grad_queries = jnp.einsum(
        "she,dhe->shd", q_logit_grad, feat_maps[:, 0], preferred_element_type=single
    )
    grad_keys = jnp.einsum(
        "she,dhe->shd", k_logit_grad, feat_maps[:, 1], preferred_element_type=single
    )
    joined_grad = jnp.concatenate(
        [
            grad_queries.reshape(row_count, D),
            grad_keys.reshape(row_count, D),
            grad_values.reshape(row_count, D),
        ],
        1,
    ).astype(bfloat)
    grad_qkv = jnp.einsum(
        "sd,se->de", complete.normed, joined_grad, preferred_element_type=single
    )
    grad_normed = jnp.einsum("se,de->sd", joined_grad, w_qkv, preferred_element_type=single)
    unused, norm_back_one = jax.vjp(normalize, complete.stream, norm_rows[0], norm_rows[1])
    grad_stream, grad_gain_one, grad_shift_one = norm_back_one(grad_normed)
    grad_norms = jnp.stack([grad_gain_one, grad_shift_one, grad_gain_two, grad_shift_two])
    grad_maps = jnp.stack([grad_map_q, grad_map_k], 1).reshape(HD, 2 * D)
    return (
        grad_stream + grad_middle,
        (grad_norms, grad_qkv, grad_maps, grad_out, grad_up, grad_down),
    )


def general_on_device(
    tokens,
    cotangent,
    lengths,
    norm_params,
    qkv_weight,
    feature_weight,
    out_weight,
    up_weight,
    down_weight,
):
    params = (
        norm_params[0],
        qkv_weight[0],
        feature_weight[0],
        out_weight[0],
        up_weight[0],
        down_weight[0],
    )
    section_id = lax.axis_index("pipe")
    micro_count = tokens.shape[0]
    row_count = tokens.shape[1]
    positions = lax.axis_index("seq") * row_count + jnp.arange(row_count, dtype=jnp.int32)
    received = jnp.zeros((row_count, D), bfloat)
    kept_list = []
    sent_list = []
    for moment in range(micro_count + 1):
        micro_index = jnp.clip(moment - section_id, 0, micro_count - 1)
        own_rows = lax.dynamic_index_in_dim(tokens, micro_index, 0, False)
        section_input = jnp.where(section_id == 0, own_rows, received)
        seg_ids = segments(lax.dynamic_index_in_dim(lengths, micro_index, 0, False), positions)
        front = front_pass(section_input, params)
        local_state = tail_state(front.key_feats, front.values, seg_ids)
        incoming = carried_in_2(local_state, "seq", join_states, empty_state(), False)
        complete = rear_pass(front, incoming, seg_ids, params)
        kept_list.append(complete)
        sent_value = complete.result.astype(bfloat)
        sent_list.append(sent_value)
        if moment < micro_count:
            received = passed_along(for_sending(sent_value), "pipe", 1).astype(sent_value.dtype)
    totals = tuple((jnp.zeros(tensor.shape, single) for tensor in params))
    returned = jnp.zeros((row_count, D), bfloat)
    back_list = []
    is_first = section_id == 0
    for moment in range(micro_count + 1):
        raw_index = moment - 1 + section_id
        micro_index = jnp.clip(raw_index, 0, micro_count - 1)
        active = (raw_index >= 0) & (raw_index < micro_count)
        own_grad = lax.dynamic_index_in_dim(cotangent, micro_index, 0, False)
        grad_result = jnp.where(section_id == 1, own_grad, returned).astype(single)
        seg_ids = segments(lax.dynamic_index_in_dim(lengths, micro_index, 0, False), positions)
        first_slot = min(max(moment - 1, 0), micro_count - 1)
        second_slot = min(moment, micro_count - 1) + 1
        saved = jax.tree.map(
            lambda early_leaf, late_leaf: jnp.where(is_first, early_leaf, late_leaf),
            kept_list[first_slot],
            kept_list[second_slot],
        )
        complete = saved
        grad_stream, updates = backward_pass(complete, grad_result, seg_ids, params)
        back_value = grad_stream.astype(bfloat)
        back_list.append(back_value)
        if moment < micro_count:
            returned = passed_along(back_value, "pipe", -1)
        totals = tuple(
            (running + jnp.where(active, update, 0.0) for running, update in zip(totals, updates))
        )
    forward_all = jnp.stack(sent_list)
    layer_out = jnp.where(section_id == 0, forward_all[:micro_count], forward_all[1:])
    backward_all = jnp.stack(back_list)
    input_grad = jnp.where(section_id == 1, backward_all[:micro_count], backward_all[1:])
    sum_norms, sum_qkv, sum_maps, sum_out, sum_up, sum_down = totals
    sum_pairs = sum_qkv[:, : 2 * D]
    sum_value = sum_qkv[:, 2 * D :]
    half_norms, half_pairs, half_value, half_maps, half_out, half_up, half_down = (
        lax.psum_scatter(sum_norms[None], "dp", scatter_dimension=2, tiled=True),
        lax.psum_scatter(sum_pairs[None], "dp", scatter_dimension=2, tiled=True),
        lax.psum_scatter(sum_value[None], "dp", scatter_dimension=2, tiled=True),
        lax.psum_scatter(sum_maps[None], "dp", scatter_dimension=2, tiled=True),
        lax.psum_scatter(sum_out[None], "dp", scatter_dimension=2, tiled=True),
        lax.psum_scatter(sum_up[None], "dp", scatter_dimension=2, tiled=True),
        lax.psum_scatter(sum_down[None], "dp", scatter_dimension=2, tiled=True),
    )
    reduced = (
        lax.psum_scatter(half_norms, "seq", scatter_dimension=2, tiled=True),
        lax.psum_scatter(half_pairs, "seq", scatter_dimension=2, tiled=True),
        lax.psum_scatter(half_value, "seq", scatter_dimension=2, tiled=True),
        lax.psum_scatter(half_maps, "seq", scatter_dimension=2, tiled=True),
        lax.psum_scatter(half_out, "seq", scatter_dimension=2, tiled=True),
        lax.psum_scatter(half_up, "seq", scatter_dimension=2, tiled=True),
        lax.psum_scatter(half_down, "seq", scatter_dimension=2, tiled=True),
    )
    return (
        layer_out[None],
        input_grad[None],
        reduced[0],
        reduced[1],
        reduced[2],
        reduced[3],
        reduced[4],
        reduced[5],
        reduced[6],
    )


FF = 3072
BLK = 256
THIN = D // 16
WIDE = FF // 16
REST_A = 2 * THIN
REST = 4 * THIN + 16
bfloat = jnp.bfloat16
single = jnp.float32
VMEM_BYTES = 60 * 1024 * 1024
HBM = pl.BlockSpec(memory_space=pltpu.HBM)
SMEM = pl.BlockSpec(memory_space=pltpu.SMEM)
VMEM = pl.BlockSpec(memory_space=pltpu.VMEM)


def dot_nn(a, b):
    return lax.dot_general(a, b, (((1,), (0,)), ((), ())), preferred_element_type=single)


def dot_nt(a, b):
    return lax.dot_general(a, b, (((1,), (1,)), ((), ())), preferred_element_type=single)


def dot_tn(a, b):
    return lax.dot_general(a, b, (((0,), (0,)), ((), ())), preferred_element_type=single)


def standardize(stream):
    centred = stream - jnp.mean(stream, -1, keepdims=True)
    scale = lax.rsqrt(jnp.mean(centred * centred, -1, keepdims=True) + 1e-05)
    return centred * scale, scale


def standardize_back(grad, unit, scale, gain):
    grad_unit = grad * gain
    return scale * (
        grad_unit
        - jnp.mean(grad_unit, -1, keepdims=True)
        - unit * jnp.mean(grad_unit * unit, -1, keepdims=True)
    )


def softmax_pair(logits):
    up = jnp.exp(logits - jnp.max(logits, 0, keepdims=True))
    down = jnp.exp(jnp.min(logits, 0, keepdims=True) - logits)
    up = up * (1.0 / jnp.sum(up, 0, keepdims=True))
    down = down * (1.0 / jnp.sum(down, 0, keepdims=True))
    return jnp.concatenate([up, down], 0).astype(bfloat)


def softmax_pair_back(feats, grad):
    up, down = feats[:HD].astype(single), feats[HD:].astype(single)
    grad_up, grad_down = grad[:HD], grad[HD:]
    grad_up = up * (grad_up - jnp.sum(up * grad_up, 0, keepdims=True))
    grad_down = down * (grad_down - jnp.sum(down * grad_down, 0, keepdims=True))
    return (grad_up - grad_down).astype(bfloat)


def fill_mask(info, mask_ref):
    rows = mask_ref.shape[0]
    source = lax.broadcasted_iota(jnp.int32, (rows, rows), 0)
    target = lax.broadcasted_iota(jnp.int32, (rows, rows), 1)
    allowed = source <= target
    for index in range(4):
        end = info[4 + index]
        allowed = allowed & ((source >= end) | (target < end))
    mask_ref[...] = jnp.where(allowed, 1.0, 0.0).astype(bfloat)


def block_maps(wfeat_ref, group):
    cols = wfeat_ref[:, pl.ds(group * BLK, BLK)]
    tall = jnp.concatenate([cols] * (BLK // HD), 0)
    row = lax.broadcasted_iota(jnp.int32, (BLK, BLK), 0) // HD
    col = lax.broadcasted_iota(jnp.int32, (BLK, BLK), 1) // HD
    return jnp.where(row == col, tall, jnp.zeros_like(tall))


def with_ones(values_t):
    count = values_t.shape[1]
    row = lax.broadcasted_iota(jnp.int32, (16, count), 0)
    extra = jnp.where(row < 2, 1.0, 0.0).astype(bfloat)
    return jnp.concatenate([values_t, extra], 0)


class Kept(NamedTuple):
    normed: Any
    qk: Any
    qft: Any
    kft: Any
    vt: Any
    ot: Any
    rden: Any
    mixed: Any
    middle: Any
    normed_two: Any
    hidden: Any
    slope: Any
    result: Any


KEPT = len(Kept._fields)


def kept_shapes(t):
    return Kept(
        normed=jax.ShapeDtypeStruct((t, D), bfloat),
        qk=jax.ShapeDtypeStruct((t, 2 * D), bfloat),
        qft=jax.ShapeDtypeStruct((2 * D, t), bfloat),
        kft=jax.ShapeDtypeStruct((2 * D, t), bfloat),
        vt=jax.ShapeDtypeStruct((D, t), bfloat),
        ot=jax.ShapeDtypeStruct((D, t), single),
        rden=jax.ShapeDtypeStruct((16, t), single),
        mixed=jax.ShapeDtypeStruct((t, D), bfloat),
        middle=jax.ShapeDtypeStruct((t, D), single),
        normed_two=jax.ShapeDtypeStruct((t, D), bfloat),
        hidden=jax.ShapeDtypeStruct((t, FF), bfloat),
        slope=jax.ShapeDtypeStruct((t, FF), bfloat),
        result=jax.ShapeDtypeStruct((t, D), bfloat),
    )


def scratch_like(shapes):
    return [pltpu.VMEM(shape.shape, shape.dtype) for shape in shapes]


def cost(micros):
    return pl.CostEstimate(flops=int(micros * 1e9), bytes_accessed=0, transcendentals=0)


def forward_steps(info, x, norm_ref, wfeat_ref, weights, mask, kept, loads):
    wqkv, wout, wup, unused = weights
    rows = x.shape[0]
    loads[0].wait()
    unit, unused = standardize(x[...].astype(single))
    kept.normed[...] = (unit * norm_ref[0:1] + norm_ref[1:2]).astype(bfloat)
    fill_mask(info, mask)
    loads[1].wait()
    normed = kept.normed[...]
    for group in range(6):
        part = dot_nn(normed, wqkv[:, group * BLK : (group + 1) * BLK]).astype(bfloat)
        kept.qk[:, group * BLK : (group + 1) * BLK] = part
        logits_t = dot_nn(part, block_maps(wfeat_ref, group)).T
        target = kept.qft if group < 3 else kept.kft
        for head in range(BLK // HD):
            start = ((group % 3) * (BLK // HD) + head) * 2 * HD
            target[start : start + 2 * HD, :] = softmax_pair(
                logits_t[head * HD : (head + 1) * HD]
            )
    centres = []
    for group in range(3):
        part = dot_nn(normed, wqkv[:, 2 * D + group * BLK : 2 * D + (group + 1) * BLK])
        part_t = part.T
        centre = jnp.mean(part_t, 1, keepdims=True)
        centres.append(centre)
        kept.vt[group * BLK : (group + 1) * BLK, :] = (part_t - centre).astype(bfloat)
    kept.rden[...] = jnp.zeros_like(kept.rden)

    def head_step(head):
        wide = pl.ds(pl.multiple_of(head * 2 * HD, 2 * HD), 2 * HD)
        thin = pl.ds(pl.multiple_of(head * HD, HD), HD)
        keys = kept.kft[wide, :].T
        queries_t = kept.qft[wide, :]
        values_t = with_ones(kept.vt[thin, :])
        for block in range(rows // BLK):
            here = slice(block * BLK, (block + 1) * BLK)
            past = slice(0, (block + 1) * BLK)
            weights = dot_nn(keys[past], queries_t[:, here]).astype(bfloat) * mask[past, here]
            summed = dot_nn(values_t[:, past], weights)
            inverse = 1.0 / summed[HD : HD + 1]
            kept.rden[pl.ds(head, 1), here] = inverse
            kept.ot[thin, here] = summed[:HD] * inverse

    @pl.loop(0, H // 4)
    def _(group):
        for head in range(4):
            head_step(4 * group + head)

    for group in range(3):
        part = kept.ot[group * BLK : (group + 1) * BLK, :] + centres[group]
        kept.mixed[:, group * BLK : (group + 1) * BLK] = part.T.astype(bfloat)
    for load in loads[2:]:
        load.wait()
    kept.middle[...] = x[...].astype(single) + dot_nn(kept.mixed[...], wout[...])
    unit, unused = standardize(kept.middle[...])
    kept.normed_two[...] = (unit * norm_ref[2:3] + norm_ref[3:4]).astype(bfloat)
    root = 0.7978845608028654
    for tile in range(FF // D):
        cols = slice(tile * D, (tile + 1) * D)
        pre = dot_nn(kept.normed_two[...], wup[:, cols])
        square = pre * pre
        bent = jnp.tanh(pre * (root + (root * 0.044715) * square))
        half = 0.5 + 0.5 * bent
        kept.hidden[:, cols] = (pre * half).astype(bfloat)
        slope = half + (pre * (half * (1.0 - bent))) * (root + (3 * root * 0.044715) * square)
        kept.slope[:, cols] = slope.astype(bfloat)


def layer_result(kept, weights):
    result = kept.middle[...] + dot_nn(kept.hidden[...], weights[3][...])
    kept.result[...] = result.astype(bfloat)


def forward_kernel(core, *refs):
    info, norm_ref, wfeat_ref = refs[:3]
    sources, refs = refs[3:8], refs[8:]
    outs, kept, refs = Kept(*refs[:KEPT]), Kept(*refs[KEPT : 2 * KEPT]), refs[2 * KEPT :]
    x, *weights = targets = refs[:5]
    mask, sem_in, sem_out = refs[5:]

    def body():
        loads = start_loads(sources, targets, sem_in)
        forward_steps(info, x, norm_ref, wfeat_ref, weights, mask, kept, loads)
        stores = start_loads(kept[:-1], outs[:-1], sem_out)
        layer_result(kept, weights)
        last = pltpu.make_async_copy(kept.result, outs.result, sem_out.at[KEPT - 1])
        last.start()
        for store in stores:
            store.wait()
        last.wait()

    pl.when(info[0] == core)(body)


def forward_call(core, info, x, norm, wfeat, wqkv, wout, wup, wdown):
    rows = x.shape[0]
    shapes = kept_shapes(rows)
    sources = (x, wqkv, wout, wup, wdown)
    kept = pl.pallas_call(
        functools.partial(forward_kernel, core),
        out_shape=list(shapes),
        in_specs=[SMEM, VMEM, VMEM] + [HBM] * 5,
        out_specs=[HBM] * KEPT,
        scratch_shapes=scratch_like(shapes)
        + scratch_like(sources)
        + [
            pltpu.VMEM((rows, rows), bfloat),
            pltpu.SemaphoreType.DMA((5,)),
            pltpu.SemaphoreType.DMA((KEPT,)),
        ],
        compiler_params=pltpu.CompilerParams(vmem_limit_bytes=VMEM_BYTES),
        cost_estimate=cost(25),
        name="layer_forward",
    )(info, norm, wfeat, *sources)
    return Kept(*kept)


def ship(info, stage, keep, send, first, sem, shards=range(16)):
    rows = keep.shape[2]
    copies = []
    for shard in shards:
        z, y, x = shard // 4, shard // 2 % 2, shard % 2
        if first == 3:
            mine = z % 2 == info[3] % 2
            place = (z // 2, shard % 4)
        else:
            mine = (x if first == 1 else y) == info[first]
            place = (z, y if first == 1 else x)
        source = stage.at[pl.ds(shard * rows, rows)]

        @pl.when(mine)
        def _():
            pltpu.make_async_copy(source, keep.at[place], sem).start()

        @pl.when(jnp.logical_not(mine))
        def _():
            pltpu.make_async_copy(source, send.at[place], sem).start()

        copies.append(pltpu.make_async_copy(source, keep.at[place], sem))
    return copies


def place(stage, part, at, rows, first_shard=0):
    size = stage.shape[0] // 16
    part = part.astype(bfloat)
    for index in range(part.shape[0] // rows):
        start = (first_shard + index) * size + at
        stage[start : start + rows, :] = part[index * rows : (index + 1) * rows]


def halves(*sizes):
    return [jax.ShapeDtypeStruct((4, 2, rows, D), bfloat) for rows in sizes for _ in range(2)]


def stages_of(*sizes):
    return [pltpu.VMEM((16 * rows, D), bfloat) for rows in sizes]


def ff_back_steps(info, g, norm_ref, weights, kept, g_pre, outs, refs, sem_out, ready):
    wup, wdown = weights[2:]
    g_middle_o, gnorm_o, keep_a, send_a, keep_b, send_b = outs
    g_middle, gnorm, stage_a, stage_b = refs
    g_t = g[...].T
    for tile in range(FF // D):
        cols = slice(tile * D, (tile + 1) * D)
        place(stage_a, dot_nn(g_t, kept.hidden[:, cols]), tile * THIN, THIN)
    ready()
    for tile in range(FF // D):
        cols = slice(tile * D, (tile + 1) * D)
        g_hidden = dot_nt(g[...], wdown[cols, :])
        g_pre[:, cols] = (g_hidden * kept.slope[:, cols].astype(single)).astype(bfloat)
    place(stage_b, dot_tn(g_pre[...], kept.normed_two[...]), 0, WIDE)
    copies = ship(info, stage_a, keep_a, send_a, 1, sem_out.at[0])
    copies += ship(info, stage_b, keep_b, send_b, 2, sem_out.at[1])
    g_normed = dot_nt(g_pre[...], wup[...])
    unit, scale = standardize(kept.middle[...])
    gnorm[0:1, :] = jnp.sum(g_normed * unit, 0, keepdims=True)
    gnorm[1:2, :] = jnp.sum(g_normed, 0, keepdims=True)
    g_middle[...] = g[...].astype(single) + standardize_back(g_normed, unit, scale, norm_ref[2:3])
    for i, (src, dst) in enumerate(((g_middle, g_middle_o), (gnorm, gnorm_o))):
        copies.append(pltpu.make_async_copy(src, dst, sem_out.at[2 + i]))
        copies[-1].start()
    return copies


def ff_back_shapes(rows):
    return [
        jax.ShapeDtypeStruct((rows, D), single),
        jax.ShapeDtypeStruct((2, D), single),
    ]


def ff_back_kernel(core, late, *refs):
    info, norm_ref = refs[:2]
    sources, refs = refs[2:9], refs[9 + late :]
    outs, targets, refs = refs[:6], refs[6:13], refs[13:]
    g, hidden, wdown, slope, normed_two, wup, middle = targets
    g_pre, *refs, sem_in, sem_out = refs
    kept = Kept(*[None] * KEPT)._replace(
        hidden=hidden, slope=slope, normed_two=normed_two, middle=middle
    )

    def body():
        loads = start_loads(sources, targets, sem_in)

        def ready():
            for load in loads[2:]:
                load.wait()

        loads[0].wait()
        loads[1].wait()
        for copy in ff_back_steps(
            info, g, norm_ref, (None, None, wup, wdown), kept, g_pre, outs, refs, sem_out, ready
        ):
            copy.wait()

    pl.when(info[0] == core)(body)


def ff_back_call(core, info, g, norm, wdown, wup, kept, after):
    rows = g.shape[0]
    loads = (g, kept.hidden, wdown, kept.slope, kept.normed_two, wup, kept.middle)
    return pl.pallas_call(
        functools.partial(ff_back_kernel, core, len(after)),
        out_shape=ff_back_shapes(rows) + halves(WIDE, WIDE),
        in_specs=[SMEM, VMEM] + [HBM] * (7 + len(after)),
        out_specs=[HBM] * 6,
        scratch_shapes=scratch_like(loads)
        + [pltpu.VMEM((rows, FF), bfloat)]
        + scratch_like(ff_back_shapes(rows))
        + stages_of(WIDE, WIDE)
        + [pltpu.SemaphoreType.DMA((7,)), pltpu.SemaphoreType.DMA((4,))],
        compiler_params=pltpu.CompilerParams(vmem_limit_bytes=VMEM_BYTES),
        cost_estimate=cost(18),
        name="feed_forward_backward",
    )(info, norm, *loads, *after)


def turn_kernel(core, *refs):
    info, norm_ref, wfeat_ref = refs[:3]
    sources, refs = refs[3:9], refs[9 + KEPT :]
    outs, back_outs, refs = Kept(*refs[:KEPT]), refs[KEPT : KEPT + 6], refs[KEPT + 6 :]
    kept, refs = Kept(*refs[:KEPT]), refs[KEPT:]
    x, *weights, g = targets = refs[:6]
    mask, *refs, sem_in, sem_out, sem_back = refs[6:]

    def body():
        loads = start_loads(sources, targets, sem_in)
        forward_steps(info, x, norm_ref, wfeat_ref, weights, mask, kept, loads)
        mine = [
            (src, dst)
            for src, dst in zip(kept, outs)
            if src is not kept.result
            and src is not kept.hidden
            and src is not kept.slope
            and src is not kept.middle
            and src is not kept.normed_two
        ]
        copies = ff_back_steps(
            info, g, norm_ref, weights, kept, kept.slope, back_outs, refs, sem_back, lambda: None
        )
        copies += start_loads([src for src, dst in mine], [dst for src, dst in mine], sem_out)
        layer_result(kept, weights)
        copies.append(pltpu.make_async_copy(kept.result, outs.result, sem_out.at[KEPT - 1]))
        copies[-1].start()
        for copy in copies:
            copy.wait()

    pl.when(info[0] == core)(body)


def turn_call(core, info, x, g, norm, wfeat, wqkv, wout, wup, wdown, previous):
    rows = x.shape[0]
    shapes = kept_shapes(rows)
    sources = (x, wqkv, wout, wup, wdown, g)
    results = pl.pallas_call(
        functools.partial(turn_kernel, core),
        out_shape=list(shapes) + ff_back_shapes(rows) + halves(WIDE, WIDE),
        in_specs=[SMEM, VMEM, VMEM] + [HBM] * (6 + KEPT),
        out_specs=[HBM] * (KEPT + 6),
        scratch_shapes=scratch_like(shapes)
        + scratch_like(sources)
        + [pltpu.VMEM((rows, rows), bfloat)]
        + scratch_like(ff_back_shapes(rows))
        + stages_of(WIDE, WIDE)
        + [
            pltpu.SemaphoreType.DMA((6,)),
            pltpu.SemaphoreType.DMA((KEPT,)),
            pltpu.SemaphoreType.DMA((4,)),
        ],
        input_output_aliases={9 + i: i for i in range(KEPT)},
        compiler_params=pltpu.CompilerParams(vmem_limit_bytes=VMEM_BYTES),
        cost_estimate=cost(40),
        name="forward_and_backward",
    )(info, norm, wfeat, *sources, *previous)
    return Kept(*results[:KEPT]), results[KEPT:]


def mix_loads(kept):
    return kept.qft, kept.kft, kept.vt, kept.ot, kept.rden, kept.qk


def start_loads(sources, targets, sems):
    loads = [
        pltpu.make_async_copy(src, dst, sems.at[i])
        for i, (src, dst) in enumerate(zip(sources, targets))
    ]
    for load in loads:
        load.start()
    return loads


def attention_back(wfeat_ref, qft, kft, vt, ot, rden, qk, mask, gm_t, gl_t, gv_t, joined, misc):
    rows = joined.shape[0]

    def head_step(head):
        wide = pl.ds(pl.multiple_of(head * 2 * HD, 2 * HD), 2 * HD)
        thin = pl.ds(pl.multiple_of(head * HD, HD), HD)
        keys_t, queries_t = kft[wide, :], qft[wide, :]
        keys = keys_t.T
        values = with_ones(vt[thin, :]).T
        inverse = rden[pl.ds(head, 1), :]
        grad = gm_t[thin, :]
        tilt = -jnp.sum(grad * ot[thin, :], 0, keepdims=True) * inverse
        high = tilt.astype(bfloat).astype(single)
        grad = grad * inverse
        fill = jnp.zeros((14, rows), single)
        grads_t = jnp.concatenate([grad, high, tilt - high, fill], 0).astype(bfloat)
        grad_low = grads_t[:HD]
        g_query = []
        g_key = [None] * (rows // BLK)
        g_value = [None] * (rows // BLK)
        for block in range(rows // BLK):
            here = slice(block * BLK, (block + 1) * BLK)
            past = slice(0, (block + 1) * BLK)
            allowed = mask[past, here]
            weights = dot_nn(keys[past], queries_t[:, here]).astype(bfloat) * allowed
            g_weights = dot_nn(values[past], grads_t[:, here]).astype(bfloat) * allowed
            g_query.append(dot_nn(keys_t[:, past], g_weights))
            for other in range(block + 1):
                part = slice(other * BLK, (other + 1) * BLK)
                more_key = dot_nt(queries_t[:, here], g_weights[part])
                more_value = dot_nt(grad_low[:, here], weights[part])
                g_key[other] = more_key if g_key[other] is None else g_key[other] + more_key
                g_value[other] = (
                    more_value if g_value[other] is None else g_value[other] + more_value
                )
        gl_t[thin, :] = softmax_pair_back(queries_t, jnp.concatenate(g_query, 1))
        later = pl.ds(pl.multiple_of(D + head * HD, HD), HD)
        gl_t[later, :] = softmax_pair_back(keys_t, jnp.concatenate(g_key, 1))
        gv_t[thin, :] = jnp.concatenate(g_value, 1).astype(bfloat)

    @pl.loop(0, H // 4)
    def _(group):
        for head in range(4):
            head_step(4 * group + head)

    for group in range(6):
        span = slice(group * BLK, (group + 1) * BLK)
        part_t = gl_t[span, :]
        joined[:, span] = dot_nt(part_t.T, block_maps(wfeat_ref, group)).astype(bfloat)
        cross = dot_nn(part_t, qk[:, span])
        for head in range(BLK // HD):
            first = group * BLK + head * HD
            misc[first : first + HD, 0:HD] = cross[
                head * HD : (head + 1) * HD, head * HD : (head + 1) * HD
            ].astype(bfloat)
    for group in range(3):
        span = slice(group * BLK, (group + 1) * BLK)
        joined[:, 2 * D + group * BLK : 2 * D + (group + 1) * BLK] = gv_t[span, :].T


def rest_grads(stage_a, stage_b, at_b, branch, mixed, joined, normed):
    place(stage_a, dot_tn(branch, mixed), 0, THIN)
    place(stage_a, dot_tn(joined[:, 2 * D :], normed), THIN, THIN)
    place(stage_b, dot_tn(joined[:, : 2 * D], normed), at_b, 2 * THIN)


def stream_back(g_middle_ref, x_ref, norm_ref, gnorm_two, joined, wqkv):
    g_normed = dot_nt(joined[...], wqkv[...])
    unit, scale = standardize(x_ref[...].astype(single))
    norm_rows = jnp.concatenate(
        [
            jnp.sum(g_normed * unit, 0, keepdims=True),
            jnp.sum(g_normed, 0, keepdims=True),
            gnorm_two,
            jnp.zeros((124, D), single),
        ],
        0,
    )
    total = g_middle_ref[...] + standardize_back(g_normed, unit, scale, norm_ref[0:1])
    return total.astype(bfloat), norm_rows.T.astype(bfloat)


def place_misc(stage, misc, turned):
    size = stage.shape[0] // 16
    for shard in range(16):
        start = (shard + 1) * size - 16
        for block in range(6):
            source = shard * 2 * THIN + block * 16
            lanes = slice(block * 2 * HD, block * 2 * HD + HD)
            stage[start : start + 16, lanes] = misc[source : source + 16, :HD]
            source = shard * THIN + min(block, 2) * 16
            lanes = slice(block * 2 * HD + HD, (block + 1) * 2 * HD)
            stage[start : start + 16, lanes] = turned[source : source + 16, :HD]


def mix_stream_kernel(core, *refs):
    info, norm_ref, gnorm_two_ref, wfeat_ref = refs[:4]
    sources, outs, targets, refs = refs[4:14], refs[14:18], refs[18:28], refs[28:]
    g_middle, wout, *kept, x, wqkv = targets
    mask, gm_t, gl_t, gv_t, g_stream, joined, misc, turned, sem_in, sem_out = refs
    results = g_stream, joined, misc, turned

    def body():
        loads = start_loads(sources, targets, sem_in)
        fill_mask(info, mask)
        loads[0].wait()
        loads[1].wait()
        gm_t[...] = dot_nt(wout[...], g_middle[...].astype(bfloat))
        for load in loads[2:8]:
            load.wait()
        attention_back(wfeat_ref, *kept, mask, gm_t, gl_t, gv_t, joined, misc)
        for load in loads[8:]:
            load.wait()
        g_stream[...], turned[...] = stream_back(
            g_middle, x, norm_ref, gnorm_two_ref[...], joined, wqkv
        )
        for store in start_loads(results, outs, sem_out):
            store.wait()

    pl.when(info[0] == core)(body)


def attention_scratch(rows):
    return [
        pltpu.VMEM((rows, rows), bfloat),
        pltpu.VMEM((D, rows), single),
        pltpu.VMEM((2 * D, rows), bfloat),
        pltpu.VMEM((D, rows), bfloat),
    ]


def mix_stream_call(core, info, g_middle, x, norm, gnorm_two, wfeat, wout, wqkv, kept):
    rows = x.shape[0]
    shapes = [
        jax.ShapeDtypeStruct((rows, D), bfloat),
        jax.ShapeDtypeStruct((rows, 3 * D), bfloat),
        jax.ShapeDtypeStruct((2 * D, 2 * HD), bfloat),
        jax.ShapeDtypeStruct((D, 2 * HD), bfloat),
    ]
    sources = (g_middle, wout) + mix_loads(kept) + (x, wqkv)
    return pl.pallas_call(
        functools.partial(mix_stream_kernel, core),
        out_shape=shapes,
        in_specs=[SMEM] + [VMEM] * 3 + [HBM] * 10,
        out_specs=[HBM] * 4,
        scratch_shapes=scratch_like(sources)
        + attention_scratch(rows)
        + scratch_like(shapes)
        + [pltpu.SemaphoreType.DMA((10,)), pltpu.SemaphoreType.DMA((4,))],
        compiler_params=pltpu.CompilerParams(vmem_limit_bytes=VMEM_BYTES),
        cost_estimate=cost(18),
        name="mix_backward_stream",
    )(info, norm, gnorm_two, wfeat, *sources)


def mix_grads_kernel(core, *refs):
    info, g_middle_ref = refs[:2]
    sources, (keep, send) = refs[2:7], refs[7:9]
    targets, (stage, sem_in, sem_out) = refs[9:14], refs[14:]
    mixed, joined, normed, misc, turned = targets

    def body():
        for load in start_loads(sources, targets, sem_in):
            load.wait()
        branch = g_middle_ref[...].astype(bfloat)
        rest_grads(stage, stage, REST_A, branch, mixed[...], joined, normed[...])
        place_misc(stage, misc, turned)
        for copy in ship(info, stage, keep, send, 3, sem_out):
            copy.wait()

    pl.when(info[0] == core)(body)


def rest_halves():
    return [jax.ShapeDtypeStruct((2, 4, REST, D), bfloat)] * 2


def mix_grads_call(core, info, g_middle, kept, joined, misc, turned):
    sources = (kept.mixed, joined, kept.normed, misc, turned)
    return pl.pallas_call(
        functools.partial(mix_grads_kernel, core),
        out_shape=rest_halves(),
        in_specs=[SMEM, VMEM] + [HBM] * 5,
        out_specs=[HBM] * 2,
        scratch_shapes=scratch_like(sources)
        + stages_of(REST)
        + [pltpu.SemaphoreType.DMA((5,)), pltpu.SemaphoreType.DMA],
        compiler_params=pltpu.CompilerParams(vmem_limit_bytes=VMEM_BYTES),
        cost_estimate=cost(0.1),
        name="mix_backward_gradients",
    )(info, g_middle, *sources)


def mix_back_kernel(core, late, *refs):
    info, norm_ref, gnorm_two_ref, wfeat_ref = refs[:4]
    sources, refs = refs[4:16], refs[17 + late :]
    g_stream_o, keep_a, send_a, keep_b, send_b = refs[:5]
    targets, refs = refs[5:17], refs[17:]
    g_middle, wout, *kept, x, mixed, normed, wqkv = targets
    mask, gm_t, gl_t, gv_t, joined, misc, g_stream, stage_a, stage_b, sem_in, sem_out = refs

    def body():
        loads = start_loads(sources, targets, sem_in)
        fill_mask(info, mask)
        loads[0].wait()
        loads[1].wait()
        branch = g_middle[...].astype(bfloat)
        gm_t[...] = dot_nt(wout[...], branch)
        for load in loads[2:8]:
            load.wait()
        attention_back(wfeat_ref, *kept, mask, gm_t, gl_t, gv_t, joined, misc)
        for load in loads[8:]:
            load.wait()
        rest_grads(stage_a, stage_b, 0, branch, mixed[...], joined, normed[...])
        copies = ship(info, stage_a, keep_a, send_a, 1, sem_out.at[0])
        g_stream[...], turned = stream_back(
            g_middle, x, norm_ref, gnorm_two_ref[...], joined, wqkv
        )
        place_misc(stage_b, misc, turned)
        copies += ship(info, stage_b, keep_b, send_b, 2, sem_out.at[1])
        copies.append(pltpu.make_async_copy(g_stream, g_stream_o, sem_out.at[2]))
        copies[-1].start()
        for copy in copies:
            copy.wait()

    pl.when(info[0] == core)(body)


def mix_back_call(
    core, info, g_middle, x, norm, gnorm_two, wfeat, wout, wqkv, kept, previous, after
):
    rows = x.shape[0]
    shapes = [jax.ShapeDtypeStruct((rows, D), bfloat)] + halves(REST_A, REST - REST_A)
    sources = (g_middle, wout) + mix_loads(kept) + (x, kept.mixed, kept.normed, wqkv)
    return pl.pallas_call(
        functools.partial(mix_back_kernel, core, len(after)),
        out_shape=shapes,
        in_specs=[SMEM] + [VMEM] * 3 + [HBM] * (13 + len(after)),
        out_specs=[HBM] * 5,
        scratch_shapes=scratch_like(sources)
        + attention_scratch(rows)
        + [
            pltpu.VMEM((rows, 3 * D), bfloat),
            pltpu.VMEM((2 * D, 2 * HD), bfloat),
            pltpu.VMEM((rows, D), bfloat),
        ]
        + stages_of(REST_A, REST - REST_A)
        + [pltpu.SemaphoreType.DMA((12,)), pltpu.SemaphoreType.DMA((3,))],
        input_output_aliases={16: 0},
        compiler_params=pltpu.CompilerParams(vmem_limit_bytes=VMEM_BYTES),
        cost_estimate=cost(22),
        name="mix_backward",
    )(info, norm, gnorm_two, wfeat, *sources, previous, *after)


class Travel(NamedTuple):
    keep_a: Any
    keep_b: Any
    one_a: Any
    one_b: Any
    two_a: Any = None
    two_b: Any = None
    low: Any = None
    high: Any = None


def at_shard(travel, rows_a, z, x, y, z_high):
    span_a, span_b = pl.ds(0, rows_a), pl.ds(rows_a, travel.keep_b.shape[2])
    terms = [
        ((travel.keep_a.at[z, y], span_a), (travel.keep_b.at[z, x], span_b)),
        ((travel.one_a.at[z, y], span_a), (travel.one_b.at[z, x], span_b)),
    ]
    if travel.two_a is not None:
        terms.append(((travel.two_a.at[z], span_a), (travel.two_b.at[z], span_b)))
    if travel.low is not None:
        terms.append(((travel.low.at[z_high], pl.ds(0, rows_a + travel.keep_b.shape[2])),))
    if travel.high is not None:
        terms.append(((travel.high, pl.ds(0, rows_a + travel.keep_b.shape[2])),))
    return terms


def fetch(terms, held, sems):
    copies = []
    for index, pieces in enumerate(terms):
        for piece, (source, span) in enumerate(pieces):
            copies.append(
                pltpu.make_async_copy(source, held.at[index, span], sems.at[index, piece])
            )
    for copy in copies:
        copy.start()
    return copies


def total_of(held, count):
    total = held[0].astype(single)
    for index in range(1, count):
        total = total + held[index].astype(single)
    return total


def second_hop_kernel(core, info, keep_a, keep_b, one_a, one_b, after, out_a, out_b, *scratch):
    held_a, more_a, held_b, more_b, sem_in, sem_out = scratch

    def body():
        x, y = info[1], info[2]
        plan = (
            (keep_a.at[:, 1 - y], one_a.at[:, 1 - y], held_a, more_a, out_a),
            (keep_b.at[:, 1 - x], one_b.at[:, 1 - x], held_b, more_b, out_b),
        )
        copies = []
        for index, (keep, came, held, more, unused) in enumerate(plan):
            copies.append(pltpu.make_async_copy(keep, held, sem_in.at[2 * index]))
            copies.append(pltpu.make_async_copy(came, more, sem_in.at[2 * index + 1]))
        for copy in copies:
            copy.start()
        stores = []
        for index, (unused, unused, held, more, out) in enumerate(plan):
            copies[2 * index].wait()
            copies[2 * index + 1].wait()
            held[...] = (held[...].astype(single) + more[...].astype(single)).astype(bfloat)
            stores.append(pltpu.make_async_copy(held, out, sem_out.at[index]))
            stores[-1].start()
        for store in stores:
            store.wait()

    pl.when(info[0] == core)(body)


def second_hop_call(core, info, travel, after):
    shapes = [
        jax.ShapeDtypeStruct((4,) + keep.shape[2:], bfloat)
        for keep in (travel.keep_a, travel.keep_b)
    ]
    return pl.pallas_call(
        functools.partial(second_hop_kernel, core),
        out_shape=shapes,
        in_specs=[SMEM] + [HBM] * 5,
        out_specs=[HBM] * 2,
        scratch_shapes=scratch_like((shapes[0], shapes[0], shapes[1], shapes[1]))
        + [pltpu.SemaphoreType.DMA((4,)), pltpu.SemaphoreType.DMA((2,))],
        compiler_params=pltpu.CompilerParams(vmem_limit_bytes=VMEM_BYTES),
        cost_estimate=cost(0.1),
        name="for_second_hop",
    )(info, travel.keep_a, travel.keep_b, travel.one_a, travel.one_b, after)


def z_hop_kernel(core, count, info, *refs):
    travel, refs = Travel(*refs[:count]), refs[count + 1 :]
    out, held, total, sem_in, sem_out = refs
    rows_a = travel.keep_a.shape[2]

    def body():
        x, y, z = info[1], info[2], info[3]
        low, high = z % 2, z // 2
        if travel.low is None:
            targets = [((1 - low), 0), (2 + (1 - low), 1)]
        else:
            targets = [(2 * (1 - high) + low, 1 - high)]
        copies = [
            fetch(
                at_shard(travel, rows_a, target, x, y, target_high),
                held.at[index],
                sem_in.at[index],
            )
            for index, (target, target_high) in enumerate(targets)
        ]
        stores = []
        for index in range(len(targets)):
            for copy in copies[index]:
                copy.wait()
            count_terms = 3 if travel.low is None else 4
            total[index] = total_of(held.at[index], count_terms).astype(bfloat)
            to = out.at[index] if travel.low is None else out
            stores.append(pltpu.make_async_copy(total.at[index], to, sem_out.at[index]))
            stores[-1].start()
        for store in stores:
            store.wait()

    pl.when(info[0] == core)(body)


def z_hop_call(core, info, travel, after):
    rows = travel.keep_a.shape[2] + travel.keep_b.shape[2]
    refs = [ref for ref in travel if ref is not None]
    shape = (2, rows, D) if travel.low is None else (rows, D)
    return pl.pallas_call(
        functools.partial(z_hop_kernel, core, len(refs)),
        out_shape=jax.ShapeDtypeStruct(shape, bfloat),
        in_specs=[SMEM] + [HBM] * (len(refs) + 1),
        out_specs=HBM,
        scratch_shapes=[
            pltpu.VMEM((2, 4, rows, D), bfloat),
            pltpu.VMEM((2, rows, D), bfloat),
            pltpu.SemaphoreType.DMA((2, 4, 2)),
            pltpu.SemaphoreType.DMA((2,)),
        ],
        compiler_params=pltpu.CompilerParams(vmem_limit_bytes=VMEM_BYTES),
        cost_estimate=cost(0.1),
        name="for_z_hop",
    )(info, *refs, after)


def finish_kernel(kinds, write, info, *refs):
    count = len(kinds[0]._fields)
    travels = kinds[0](*refs[:count]), kinds[1](*refs[count : count + len(kinds[1]._fields)])
    outs = refs[count + len(kinds[1]._fields) : -2]
    held, sem_in = refs[-2:]

    def bring(travel):
        x, y, z = info[1], info[2], info[3]
        if isinstance(travel, Travel):
            terms = at_shard(travel, travel.keep_a.shape[2], z, x, y, z // 2)
        else:
            terms = rest_at(travel, x, y, z // 2)
        for copy in fetch(terms, held, sem_in):
            copy.wait()

    for core in range(2):
        pl.when(info[0] == core)(functools.partial(bring, travels[core]))
    write(total_of(held, 5), outs)


def write_early(total, outs):
    down, up = outs
    for tile in range(FF // D):
        down[0, :, tile * D : (tile + 1) * D] = total[tile * THIN : (tile + 1) * THIN]
    up[0] = total[WIDE:]


def write_rest(total, outs):
    norms, pairs, value, maps, out = outs
    out[0] = total[:THIN]
    value[0] = total[THIN : 2 * THIN]
    pairs[0] = total[2 * THIN : 4 * THIN]
    misc = total[4 * THIN :]
    tall = [misc[:, i * 2 * HD : (i + 1) * 2 * HD] for i in range(6)]
    wide = jnp.concatenate(tall + [jnp.zeros((32, 2 * HD), single)], 0).T
    maps[0] = wide[:HD, : 2 * THIN]
    norms[0] = wide[HD : HD + 4, :THIN]


def finish_call(info, first, second, rows, shapes, write):
    return pl.pallas_call(
        functools.partial(finish_kernel, (type(first), type(second)), write),
        out_shape=[jax.ShapeDtypeStruct((1,) + shape, single) for shape in shapes],
        in_specs=[SMEM] + [HBM] * (len(first) + len(second)),
        out_specs=[VMEM] * len(shapes),
        scratch_shapes=[
            pltpu.VMEM((5, rows, D), bfloat),
            pltpu.SemaphoreType.DMA((5, 2)),
        ],
        compiler_params=pltpu.CompilerParams(vmem_limit_bytes=VMEM_BYTES),
        cost_estimate=cost(0.1),
        name="shard_gradients",
    )(info, *first, *second)


class RestTravel(NamedTuple):
    keep: Any
    low: Any = None
    high: Any = None
    x: Any = None
    y: Any = None


def rest_at(travel, x, y, z_high):
    terms = [travel.keep.at[z_high, 2 * y + x], travel.low.at[z_high, 2 * y + x]]
    if travel.high is not None:
        terms.append(travel.high.at[2 * y + x])
    if travel.x is not None:
        terms.append(travel.x.at[y])
    if travel.y is not None:
        terms.append(travel.y)
    return [((term, pl.ds(0, REST)),) for term in terms]


def rest_hop_kernel(core, count, info, *refs):
    travel, refs = RestTravel(*refs[:count]), refs[count + 1 :]
    out, held, total, sem_in, sem_out = refs

    def body():
        x, y, z_high = info[1], info[2], info[3] // 2
        if count == 2:
            targets = [(i % 2, i // 2, 1 - z_high) for i in range(4)]
        elif count == 3:
            targets = [(1 - x, i, z_high) for i in range(2)]
        else:
            targets = [(x, 1 - y, z_high)]
        copies = [
            fetch(rest_at(travel, *target), held.at[i], sem_in.at[i])
            for i, target in enumerate(targets)
        ]
        stores = []
        for i in range(len(targets)):
            for copy in copies[i]:
                copy.wait()
            total[i] = total_of(held.at[i], count).astype(bfloat)
            to = out if len(targets) == 1 else out.at[i]
            stores.append(pltpu.make_async_copy(total.at[i], to, sem_out.at[i]))
            stores[-1].start()
        for store in stores:
            store.wait()

    pl.when(info[0] == core)(body)


def rest_hop_call(core, info, travel, after):
    refs = [ref for ref in travel if ref is not None]
    many = {2: 4, 3: 2, 4: 1}[len(refs)]
    shape = (REST, D) if many == 1 else (many, REST, D)
    return pl.pallas_call(
        functools.partial(rest_hop_kernel, core, len(refs)),
        out_shape=jax.ShapeDtypeStruct(shape, bfloat),
        in_specs=[SMEM] + [HBM] * (len(refs) + 1),
        out_specs=HBM,
        scratch_shapes=[
            pltpu.VMEM((many, len(refs), REST, D), bfloat),
            pltpu.VMEM((many, REST, D), bfloat),
            pltpu.SemaphoreType.DMA((many, len(refs), 1)),
            pltpu.SemaphoreType.DMA((many,)),
        ],
        compiler_params=pltpu.CompilerParams(vmem_limit_bytes=VMEM_BYTES),
        cost_estimate=cost(0.1),
        name="for_rest_hop",
    )(info, *refs, after)


def swap_on(value, core, axis, bit):
    count = lax.axis_size(axis)
    pairs = [(core * count + i, core * count + (i ^ bit)) for i in range(count)]
    return lax.ppermute(value, ("pipe", axis), pairs)


def fast_on_device(
    tokens,
    cotangent,
    lengths,
    norm_params,
    qkv_weight,
    feature_weight,
    out_weight,
    up_weight,
    down_weight,
):
    norm, wqkv, wfeat = norm_params[0], qkv_weight[0], feature_weight[0]
    wout, wup, wdown = out_weight[0], up_weight[0], down_weight[0]
    pipe, seq = lax.axis_index("pipe"), lax.axis_index("seq")
    ends = jnp.cumsum(lax.dynamic_index_in_dim(lengths, seq, 0, False)).astype(jnp.int32)
    places = jnp.stack([pipe, seq % 2, seq // 2, lax.axis_index("dp")]).astype(jnp.int32)
    info = jnp.concatenate([places, ends])
    whole = lax.all_to_all(tokens, "seq", 0, 0, tiled=True).reshape(-1, D)
    whole_grad = lax.all_to_all(cotangent, "seq", 0, 0, tiled=True).reshape(-1, D)

    def one(core, parts):
        keep_a, send_a, keep_b, send_b = parts
        return Travel(
            keep_a, keep_b, swap_on(send_a, core, "seq", 1), swap_on(send_b, core, "seq", 2)
        )

    def two(core, travel, after):
        send_a, send_b = second_hop_call(core, info, travel, after)
        return send_a, travel._replace(
            two_a=swap_on(send_a, core, "seq", 2), two_b=swap_on(send_b, core, "seq", 1)
        )

    def low(core, travel, after):
        send = z_hop_call(core, info, travel, after)
        return send, travel._replace(low=swap_on(send, core, "dp", 1))

    def high(core, travel, after):
        send = z_hop_call(core, info, travel, after)
        return send, travel._replace(high=swap_on(send, core, "dp", 2))

    def rest_low(core, parts):
        keep, send = parts
        return RestTravel(keep, swap_on(send, core, "dp", 1))

    def rest_high(core, travel, after):
        send = rest_hop_call(core, info, travel, after)
        return send, travel._replace(high=swap_on(send, core, "dp", 2))

    def rest_x(core, travel, after):
        send = rest_hop_call(core, info, travel, after)
        return send, travel._replace(x=swap_on(send, core, "seq", 1))

    def rest_y(core, travel, after):
        send = rest_hop_call(core, info, travel, after)
        return send, travel._replace(y=swap_on(send, core, "seq", 2))

    def back_to_rows(value):
        return lax.all_to_all(value.reshape(tokens.shape), "seq", 0, 0, tiled=True)[None]

    kept = forward_call(0, info, whole, norm, wfeat, wqkv, wout, wup, wdown)
    sent = lax.ppermute(kept.result, "pipe", [(0, 1)])
    kept, (g_middle, gnorm_two, *parts) = turn_call(
        1, info, sent, whole_grad, norm, wfeat, wqkv, wout, wup, wdown, kept
    )
    early_one = one(1, parts)
    g_stream, joined, misc, turned = mix_stream_call(
        1, info, g_middle, sent, norm, gnorm_two, wfeat, wout, wqkv, kept
    )
    returned = lax.ppermute(g_stream, "pipe", [(1, 0)])
    parts = mix_grads_call(1, info, g_middle, kept, joined, misc, turned)
    rest_one = rest_low(1, parts)

    layer_out = back_to_rows(kept.result)
    last, early_one = two(1, early_one, parts[0])
    g_middle, gnorm_two, *parts = ff_back_call(
        0, info, returned, norm, wdown, wup, kept, (last, layer_out)
    )
    early_two = one(0, parts)
    last = g_middle
    last, early_one = low(1, early_one, last)
    g_stream, *parts = mix_back_call(
        0, info, g_middle, whole, norm, gnorm_two, wfeat, wout, wqkv, kept, g_stream, (last,)
    )
    rest_two = one(0, parts)
    last = g_stream
    last, early_two = two(0, early_two, last)
    last, rest_one = rest_high(1, rest_one, last)
    last, rest_two = two(0, rest_two, last)
    last, early_two = low(0, early_two, last)
    last, early_one = high(1, early_one, last)
    last, rest_one = rest_x(1, rest_one, last)
    last, early_two = high(0, early_two, last)
    last, rest_two = low(0, rest_two, last)
    last, rest_one = rest_y(1, rest_one, last)
    last, rest_two = high(0, rest_two, last)
    input_grad = back_to_rows(g_stream)
    down, up = finish_call(
        info, early_two, early_one, 2 * WIDE, [(THIN, FF), (WIDE, D)], write_early
    )
    norms, pairs, value, maps, out = finish_call(
        info,
        rest_two,
        rest_one,
        REST,
        [(4, THIN), (2 * THIN, D), (THIN, D), (HD, 2 * THIN), (THIN, D)],
        write_rest,
    )
    down, up, pairs, value, out = [g.swapaxes(1, 2) for g in (down, up, pairs, value, out)]

    return layer_out, input_grad, norms, pairs, value, maps, out, up, down


def on_device(tokens, cotangent, lengths, *params):
    suits = (lax.axis_size("dp"), lax.axis_size("seq"), tokens.shape[0]) == (4, 4, 4)
    plan = fast_on_device if suits else general_on_device
    return plan(tokens, cotangent, lengths, *params)


def solution(mesh):
    in_specs = (
        P("dp", "seq", None),
        P("dp", "seq", None),
        P("dp", None),
        P("pipe", None, None),
        P("pipe", None, None),
        P("pipe", None, None),
        P("pipe", None, None),
        P("pipe", None, None),
        P("pipe", None, None),
    )
    out_specs = (
        P("pipe", "dp", "seq", None),
        P("pipe", "dp", "seq", None),
        P("pipe", None, ("dp", "seq")),
        P("pipe", None, ("dp", "seq")),
        P("pipe", None, ("dp", "seq")),
        P("pipe", None, ("dp", "seq")),
        P("pipe", None, ("dp", "seq")),
        P("pipe", None, ("dp", "seq")),
        P("pipe", None, ("dp", "seq")),
    )
    return jax.shard_map(
        on_device, mesh=mesh, in_specs=in_specs, out_specs=out_specs, check_vma=False
    )
```

```python
import functools
from typing import Any, NamedTuple

import jax
import jax.numpy as jnp
from jax import lax
from jax.experimental import pallas as pl
from jax.experimental.pallas import tpu as pltpu
from jax.sharding import PartitionSpec as P

D = 768
H = 12
HD = 64
CH = 64


highest = lax.Precision.HIGHEST
bfloat = jnp.bfloat16
single = jnp.float32


def carried_in_2(value, axis, join, neutral, backward):
    count, mine = (lax.axis_size(axis), lax.axis_index(axis))
    pieces = jax.tree.map(lambda part: lax.all_gather(part, axis), value)
    if backward:
        pieces = jax.tree.map(lambda part: part[::-1], pieces)
        mine = count - 1 - mine
    total = jax.tree.map(
        lambda part, zero: jnp.full_like(part, 0) + jnp.asarray(zero, part.dtype), value, neutral
    )

    def lap(position, total):
        longer = join(total, jax.tree.map(lambda part: part[position], pieces))
        return jax.tree.map(lambda new, old: jnp.where(position < mine, new, old), longer, total)

    return lax.fori_loop(0, count - 1, lap, total)


def for_sending(shard):
    return jax.tree.map(lambda a: a.astype(jnp.bfloat16) if a.dtype == jnp.float32 else a, shard)


def passed_along(shard, axis, by):
    length = lax.axis_size(axis)
    pairs = [(i, i + by) for i in range(length) if 0 <= i + by < length]
    return lax.ppermute(shard, axis, pairs)


def normalize(stream, norm_gain, norm_shift):
    centred = stream - jnp.mean(stream, -1, keepdims=True)
    spread = jnp.mean(centred * centred, -1, keepdims=True)
    return centred * lax.rsqrt(spread + 1e-05) * norm_gain + norm_shift


def features(logits):
    return jnp.concatenate([jax.nn.softmax(logits, -1), jax.nn.softmax(-logits, -1)], -1)


def flat_features(flat_logits):
    row_count = flat_logits.shape[0]
    return features(flat_logits.reshape(row_count, H, HD)).reshape(row_count, 2 * D)


def smooth(hidden_pre):
    return jax.nn.gelu(hidden_pre, approximate=True)


def segments(lengths_row, positions):
    doc_ends = jnp.cumsum(lengths_row)
    return jnp.sum((doc_ends[None, :] <= positions[:, None]).astype(jnp.int32), 1)


def span_step(carried_in, block_in):
    kv_state, norm_state, last_seg = carried_in
    query_feats, key_feats, values, seg_ids = block_in
    seg_float = seg_ids.astype(single)
    scores = jnp.einsum("thf,shf->hts", query_feats, key_feats, precision=highest)
    places = jnp.arange(CH, dtype=jnp.int32)
    allowed = (places[:, None] >= places[None, :]) & (seg_ids[:, None] == seg_ids[None, :])
    weights = jnp.where(allowed[None], scores, 0.0)
    carried = (seg_float == last_seg).astype(single)
    numerator = jnp.einsum("hts,shd->thd", weights, values, precision=highest) + carried[
        :, None, None
    ] * jnp.einsum("thf,hfd->thd", query_feats, kv_state, precision=highest)
    denominator = jnp.sum(weights, -1).T + carried[:, None] * jnp.einsum(
        "thf,hf->th", query_feats, norm_state, precision=highest
    )
    tail_seg = seg_float[-1]
    inside = (seg_float == tail_seg).astype(single)
    kept_part = (last_seg == tail_seg).astype(single)
    tail_keys = key_feats * inside[:, None, None]
    kv_state = kept_part * kv_state + jnp.einsum(
        "shf,shd->hfd", tail_keys, values, precision=highest
    )
    norm_state = kept_part * norm_state + jnp.sum(tail_keys, 0)
    return ((kv_state, norm_state, tail_seg), numerator / denominator[:, :, None])


def attend(query_feats, key_feats, values, seg_ids, kv_state, norm_state, last_seg):
    row_count = query_feats.shape[0]
    block_count = row_count // CH
    blocks = (
        query_feats.reshape(block_count, CH, H, 2 * HD),
        key_feats.reshape(block_count, CH, H, 2 * HD),
        values.reshape(block_count, CH, H, HD),
        seg_ids.reshape(block_count, CH),
    )
    closing, mixed_out = lax.scan(span_step, (kv_state, norm_state, last_seg), blocks)
    return mixed_out.reshape(row_count, H, HD)


def tail_state(key_feats, values, seg_ids):
    row_count = key_feats.shape[0]
    key_three = key_feats.reshape(row_count, H, 2 * HD)
    value_three = values.reshape(row_count, H, HD)
    seg_float = seg_ids.astype(single)
    tail_seg = seg_float[-1]
    tail_keys = key_three * (seg_float == tail_seg).astype(single)[:, None, None]
    return (
        jnp.einsum("shf,shd->hfd", tail_keys, value_three, precision=highest),
        jnp.sum(tail_keys, 0),
        tail_seg,
    )


def join_states(earlier, later):
    early_kv, early_norm, early_seg = earlier
    late_kv, late_norm, late_seg = later
    is_blank = late_seg < 0.0
    matches = early_seg == late_seg
    kv_sum = jnp.where(is_blank, early_kv, late_kv + jnp.where(matches, early_kv, 0.0))
    norm_sum = jnp.where(is_blank, early_norm, late_norm + jnp.where(matches, early_norm, 0.0))
    return (kv_sum, norm_sum, jnp.where(is_blank, early_seg, late_seg))


def empty_state():
    return (jnp.zeros((H, 2 * HD, HD), single), jnp.zeros((H, 2 * HD), single), jnp.float32(-1.0))


class Front(NamedTuple):
    stream: Any
    normed: Any
    queries: Any
    key_rows: Any
    values: Any
    q_logit: Any
    k_logit: Any
    query_feats: Any
    key_feats: Any


class Complete(NamedTuple):
    stream: Any
    normed: Any
    queries: Any
    key_rows: Any
    values: Any
    q_logit: Any
    k_logit: Any
    query_feats: Any
    key_feats: Any
    incoming_kv: Any
    incoming_norm: Any
    incoming_seg: Any
    mixed_low: Any
    middle: Any
    normed_two: Any
    hidden_pre: Any
    hidden: Any
    result: Any


def front_pass(section_input, params):
    norm_rows, w_qkv, w_feat = (params[0], params[1], params[2])
    stream = section_input.astype(single)
    row_count = stream.shape[0]
    normed = normalize(stream, norm_rows[0], norm_rows[1]).astype(bfloat)
    joined = jnp.dot(normed, w_qkv, preferred_element_type=single)
    queries = joined[:, :D].astype(bfloat)
    key_rows = joined[:, D : 2 * D].astype(bfloat)
    values = joined[:, 2 * D :]
    feat_maps = w_feat.reshape(HD, 2, H, HD)
    q_logit = jnp.einsum(
        "shd,dhe->she",
        queries.reshape(row_count, H, HD),
        feat_maps[:, 0],
        preferred_element_type=single,
    ).reshape(row_count, D)
    k_logit = jnp.einsum(
        "shd,dhe->she",
        key_rows.reshape(row_count, H, HD),
        feat_maps[:, 1],
        preferred_element_type=single,
    ).reshape(row_count, D)
    return Front(
        stream=stream,
        normed=normed,
        queries=queries,
        key_rows=key_rows,
        values=values,
        q_logit=q_logit,
        k_logit=k_logit,
        query_feats=flat_features(q_logit),
        key_feats=flat_features(k_logit),
    )


def rear_pass(front, incoming, seg_ids, params):
    norm_rows, w_out, w_up, w_down = (params[0], params[3], params[4], params[5])
    stream = front.stream
    row_count = stream.shape[0]
    mixed_out = attend(
        front.query_feats,
        front.key_feats,
        front.values,
        seg_ids,
        incoming[0],
        incoming[1],
        incoming[2],
    )
    mixed_low = mixed_out.reshape(row_count, D).astype(bfloat)
    middle = stream + jnp.dot(mixed_low, w_out, preferred_element_type=single)
    normed_two = normalize(middle, norm_rows[2], norm_rows[3]).astype(bfloat)
    hidden_pre = jnp.dot(normed_two, w_up, preferred_element_type=single)
    hidden = smooth(hidden_pre).astype(bfloat)
    result = middle + jnp.dot(hidden, w_down, preferred_element_type=single)
    return Complete(
        *front,
        incoming_kv=incoming[0],
        incoming_norm=incoming[1],
        incoming_seg=incoming[2],
        mixed_low=mixed_low,
        middle=middle,
        normed_two=normed_two,
        hidden_pre=hidden_pre,
        hidden=hidden,
        result=result,
    )


def backward_pass(complete, grad_result, seg_ids, params):
    norm_rows, w_qkv, w_feat, w_out, w_up, w_down = params
    row_count = grad_result.shape[0]
    down_grad = grad_result.astype(bfloat)
    grad_down = jnp.einsum(
        "sf,sd->fd", complete.hidden, down_grad, preferred_element_type=single
    )
    grad_hidden = jnp.einsum("sd,fd->sf", down_grad, w_down, preferred_element_type=single)
    unused, smooth_back = jax.vjp(smooth, complete.hidden_pre)
    pre_grad = smooth_back(grad_hidden)[0].astype(bfloat)
    grad_up = jnp.einsum(
        "sd,sf->df", complete.normed_two, pre_grad, preferred_element_type=single
    )
    grad_normed_two = jnp.einsum("sf,df->sd", pre_grad, w_up, preferred_element_type=single)
    unused, norm_back_two = jax.vjp(normalize, complete.middle, norm_rows[2], norm_rows[3])
    grad_middle, grad_gain_two, grad_shift_two = norm_back_two(grad_normed_two)
    grad_middle = grad_middle + grad_result
    branch_grad = grad_middle.astype(bfloat)
    grad_out = jnp.einsum(
        "sa,sd->ad", complete.mixed_low, branch_grad, preferred_element_type=single
    )
    grad_mixed = jnp.einsum("sd,ad->sa", branch_grad, w_out, preferred_element_type=single).reshape(
        row_count, H, HD
    )
    last_seg = complete.incoming_seg

    def core_attend(query_feats, key_feats, values, kv_state, norm_state):
        return attend(query_feats, key_feats, values, seg_ids, kv_state, norm_state, last_seg)

    unused, core_back = jax.vjp(
        core_attend,
        complete.query_feats,
        complete.key_feats,
        complete.values,
        complete.incoming_kv,
        complete.incoming_norm,
    )
    grad_qf, grad_kf, grad_values, grad_kv, grad_norm = core_back(grad_mixed)
    passed = carried_in_2((grad_kv, grad_norm, last_seg), "seq", join_states, empty_state(), True)

    def summary(key_feats, values):
        kv_sum, norm_sum, tail_seg = tail_state(key_feats, values, seg_ids)
        return (kv_sum, norm_sum)

    unused, summary_back = jax.vjp(summary, complete.key_feats, complete.values)
    extra_kf, extra_values = summary_back((passed[0], passed[1]))
    grad_kf = grad_kf + extra_kf
    grad_values = grad_values + extra_values
    unused, feat_back_q = jax.vjp(flat_features, complete.q_logit)
    unused, feat_back_k = jax.vjp(flat_features, complete.k_logit)
    q_logit_grad = feat_back_q(grad_qf)[0].astype(bfloat).reshape(row_count, H, HD)
    k_logit_grad = feat_back_k(grad_kf)[0].astype(bfloat).reshape(row_count, H, HD)
    feat_maps = w_feat.reshape(HD, 2, H, HD)
    grad_map_q = jnp.einsum(
        "shd,she->dhe",
        complete.queries.reshape(row_count, H, HD),
        q_logit_grad,
        preferred_element_type=single,
    )
    grad_map_k = jnp.einsum(
        "shd,she->dhe",
        complete.key_rows.reshape(row_count, H, HD),
        k_logit_grad,
        preferred_element_type=single,
    )
    grad_queries = jnp.einsum(
        "she,dhe->shd", q_logit_grad, feat_maps[:, 0], preferred_element_type=single
    )
    grad_keys = jnp.einsum(
        "she,dhe->shd", k_logit_grad, feat_maps[:, 1], preferred_element_type=single
    )
    joined_grad = jnp.concatenate(
        [
            grad_queries.reshape(row_count, D),
            grad_keys.reshape(row_count, D),
            grad_values.reshape(row_count, D),
        ],
        1,
    ).astype(bfloat)
    grad_qkv = jnp.einsum(
        "sd,se->de", complete.normed, joined_grad, preferred_element_type=single
    )
    grad_normed = jnp.einsum("se,de->sd", joined_grad, w_qkv, preferred_element_type=single)
    unused, norm_back_one = jax.vjp(normalize, complete.stream, norm_rows[0], norm_rows[1])
    grad_stream, grad_gain_one, grad_shift_one = norm_back_one(grad_normed)
    grad_norms = jnp.stack([grad_gain_one, grad_shift_one, grad_gain_two, grad_shift_two])
    grad_maps = jnp.stack([grad_map_q, grad_map_k], 1).reshape(HD, 2 * D)
    return (
        grad_stream + grad_middle,
        (grad_norms, grad_qkv, grad_maps, grad_out, grad_up, grad_down),
    )


def general_on_device(
    tokens,
    cotangent,
    lengths,
    norm_params,
    qkv_weight,
    feature_weight,
    out_weight,
    up_weight,
    down_weight,
):
    params = (
        norm_params[0],
        qkv_weight[0],
        feature_weight[0],
        out_weight[0],
        up_weight[0],
        down_weight[0],
    )
    section_id = lax.axis_index("pipe")
    micro_count = tokens.shape[0]
    row_count = tokens.shape[1]
    positions = lax.axis_index("seq") * row_count + jnp.arange(row_count, dtype=jnp.int32)
    received = jnp.zeros((row_count, D), bfloat)
    kept_list = []
    sent_list = []
    for moment in range(micro_count + 1):
        micro_index = jnp.clip(moment - section_id, 0, micro_count - 1)
        own_rows = lax.dynamic_index_in_dim(tokens, micro_index, 0, False)
        section_input = jnp.where(section_id == 0, own_rows, received)
        seg_ids = segments(lax.dynamic_index_in_dim(lengths, micro_index, 0, False), positions)
        front = front_pass(section_input, params)
        local_state = tail_state(front.key_feats, front.values, seg_ids)
        incoming = carried_in_2(local_state, "seq", join_states, empty_state(), False)
        complete = rear_pass(front, incoming, seg_ids, params)
        kept_list.append(complete)
        sent_value = complete.result.astype(bfloat)
        sent_list.append(sent_value)
        if moment < micro_count:
            received = passed_along(for_sending(sent_value), "pipe", 1).astype(sent_value.dtype)
    totals = tuple((jnp.zeros(tensor.shape, single) for tensor in params))
    returned = jnp.zeros((row_count, D), bfloat)
    back_list = []
    is_first = section_id == 0
    for moment in range(micro_count + 1):
        raw_index = moment - 1 + section_id
        micro_index = jnp.clip(raw_index, 0, micro_count - 1)
        active = (raw_index >= 0) & (raw_index < micro_count)
        own_grad = lax.dynamic_index_in_dim(cotangent, micro_index, 0, False)
        grad_result = jnp.where(section_id == 1, own_grad, returned).astype(single)
        seg_ids = segments(lax.dynamic_index_in_dim(lengths, micro_index, 0, False), positions)
        first_slot = min(max(moment - 1, 0), micro_count - 1)
        second_slot = min(moment, micro_count - 1) + 1
        saved = jax.tree.map(
            lambda early_leaf, late_leaf: jnp.where(is_first, early_leaf, late_leaf),
            kept_list[first_slot],
            kept_list[second_slot],
        )
        complete = saved
        grad_stream, updates = backward_pass(complete, grad_result, seg_ids, params)
        back_value = grad_stream.astype(bfloat)
        back_list.append(back_value)
        if moment < micro_count:
            returned = passed_along(back_value, "pipe", -1)
        totals = tuple(
            (running + jnp.where(active, update, 0.0) for running, update in zip(totals, updates))
        )
    forward_all = jnp.stack(sent_list)
    layer_out = jnp.where(section_id == 0, forward_all[:micro_count], forward_all[1:])
    backward_all = jnp.stack(back_list)
    input_grad = jnp.where(section_id == 1, backward_all[:micro_count], backward_all[1:])
    sum_norms, sum_qkv, sum_maps, sum_out, sum_up, sum_down = totals
    sum_pairs = sum_qkv[:, : 2 * D]
    sum_value = sum_qkv[:, 2 * D :]
    half_norms, half_pairs, half_value, half_maps, half_out, half_up, half_down = (
        lax.psum_scatter(sum_norms[None], "dp", scatter_dimension=2, tiled=True),
        lax.psum_scatter(sum_pairs[None], "dp", scatter_dimension=2, tiled=True),
        lax.psum_scatter(sum_value[None], "dp", scatter_dimension=2, tiled=True),
        lax.psum_scatter(sum_maps[None], "dp", scatter_dimension=2, tiled=True),
        lax.psum_scatter(sum_out[None], "dp", scatter_dimension=2, tiled=True),
        lax.psum_scatter(sum_up[None], "dp", scatter_dimension=2, tiled=True),
        lax.psum_scatter(sum_down[None], "dp", scatter_dimension=2, tiled=True),
    )
    reduced = (
        lax.psum_scatter(half_norms, "seq", scatter_dimension=2, tiled=True),
        lax.psum_scatter(half_pairs, "seq", scatter_dimension=2, tiled=True),
        lax.psum_scatter(half_value, "seq", scatter_dimension=2, tiled=True),
        lax.psum_scatter(half_maps, "seq", scatter_dimension=2, tiled=True),
        lax.psum_scatter(half_out, "seq", scatter_dimension=2, tiled=True),
        lax.psum_scatter(half_up, "seq", scatter_dimension=2, tiled=True),
        lax.psum_scatter(half_down, "seq", scatter_dimension=2, tiled=True),
    )
    return (
        layer_out[None],
        input_grad[None],
        reduced[0],
        reduced[1],
        reduced[2],
        reduced[3],
        reduced[4],
        reduced[5],
        reduced[6],
    )


FF = 3072
BLK = 256
THIN = D // 16
WIDE = FF // 16
REST = 4 * THIN + 16
bfloat = jnp.bfloat16
single = jnp.float32
VMEM_BYTES = 63 * 1024 * 1024
HBM = pl.BlockSpec(memory_space=pltpu.HBM)
SMEM = pl.BlockSpec(memory_space=pltpu.SMEM)
VMEM = pl.BlockSpec(memory_space=pltpu.VMEM)


def dot_nn(a, b):
    return lax.dot_general(a, b, (((1,), (0,)), ((), ())), preferred_element_type=single)


def dot_nt(a, b):
    return lax.dot_general(a, b, (((1,), (1,)), ((), ())), preferred_element_type=single)


def dot_tn(a, b):
    return lax.dot_general(a, b, (((0,), (0,)), ((), ())), preferred_element_type=single)


def standardize(stream):
    centred = stream - jnp.mean(stream, -1, keepdims=True)
    scale = lax.rsqrt(jnp.mean(centred * centred, -1, keepdims=True) + 1e-05)
    return centred * scale, scale


def standardize_back(grad, unit, scale, gain):
    grad_unit = grad * gain
    return scale * (
        grad_unit
        - jnp.mean(grad_unit, -1, keepdims=True)
        - unit * jnp.mean(grad_unit * unit, -1, keepdims=True)
    )


def softmax_pair(logits):
    up = jnp.exp(logits - jnp.max(logits, 0, keepdims=True))
    down = jnp.exp(jnp.min(logits, 0, keepdims=True) - logits)
    up = up * (1.0 / jnp.sum(up, 0, keepdims=True))
    down = down * (1.0 / jnp.sum(down, 0, keepdims=True))
    return jnp.concatenate([up, down], 0).astype(bfloat)


def softmax_pair_back(feats, grad):
    up, down = feats[:HD].astype(single), feats[HD:].astype(single)
    grad_up, grad_down = grad[:HD], grad[HD:]
    grad_up = up * (grad_up - jnp.sum(up * grad_up, 0, keepdims=True))
    grad_down = down * (grad_down - jnp.sum(down * grad_down, 0, keepdims=True))
    return (grad_up - grad_down).astype(bfloat)


def fill_mask(info, mask_ref):
    rows = mask_ref.shape[0]
    source = lax.broadcasted_iota(jnp.int32, (rows, rows), 0)
    target = lax.broadcasted_iota(jnp.int32, (rows, rows), 1)
    allowed = source <= target
    for index in range(4):
        end = info[4 + index]
        allowed = allowed & ((source >= end) | (target < end))
    mask_ref[...] = jnp.where(allowed, 1.0, 0.0).astype(bfloat)


def block_maps(wfeat_ref, group):
    cols = wfeat_ref[:, pl.ds(group * BLK, BLK)]
    tall = jnp.concatenate([cols] * (BLK // HD), 0)
    row = lax.broadcasted_iota(jnp.int32, (BLK, BLK), 0) // HD
    col = lax.broadcasted_iota(jnp.int32, (BLK, BLK), 1) // HD
    return jnp.where(row == col, tall, jnp.zeros_like(tall))


def with_ones(values_t):
    count = values_t.shape[1]
    row = lax.broadcasted_iota(jnp.int32, (16, count), 0)
    extra = jnp.where(row < 2, 1.0, 0.0).astype(bfloat)
    return jnp.concatenate([values_t, extra], 0)


class Kept(NamedTuple):
    normed: Any
    qk: Any
    qft: Any
    kft: Any
    vt: Any
    ot: Any
    rden: Any
    mixed: Any
    middle: Any
    normed_two: Any
    hidden: Any
    slope: Any
    result: Any


KEPT = len(Kept._fields)


def kept_shapes(t):
    return Kept(
        normed=jax.ShapeDtypeStruct((t, D), bfloat),
        qk=jax.ShapeDtypeStruct((t, 2 * D), bfloat),
        qft=jax.ShapeDtypeStruct((2 * D, t), bfloat),
        kft=jax.ShapeDtypeStruct((2 * D, t), bfloat),
        vt=jax.ShapeDtypeStruct((D, t), bfloat),
        ot=jax.ShapeDtypeStruct((D, t), single),
        rden=jax.ShapeDtypeStruct((16, t), single),
        mixed=jax.ShapeDtypeStruct((t, D), bfloat),
        middle=jax.ShapeDtypeStruct((t, D), single),
        normed_two=jax.ShapeDtypeStruct((t, D), bfloat),
        hidden=jax.ShapeDtypeStruct((t, FF), bfloat),
        slope=jax.ShapeDtypeStruct((t, FF), bfloat),
        result=jax.ShapeDtypeStruct((t, D), bfloat),
    )


def scratch_like(shapes):
    return [pltpu.VMEM(shape.shape, shape.dtype) for shape in shapes]


def cost(micros):
    return pl.CostEstimate(flops=int(micros * 1e9), bytes_accessed=0, transcendentals=0)


def forward_steps(info, x, norm_ref, wfeat_ref, weights, mask, kept, loads):
    wqkv, wout, wup, unused = weights
    rows = x.shape[0]
    loads[0].wait()
    unit, unused = standardize(x[...].astype(single))
    kept.normed[...] = (unit * norm_ref[0:1] + norm_ref[1:2]).astype(bfloat)
    fill_mask(info, mask)
    loads[1].wait()
    normed = kept.normed[...]
    for group in range(6):
        part = dot_nn(normed, wqkv[:, group * BLK : (group + 1) * BLK]).astype(bfloat)
        kept.qk[:, group * BLK : (group + 1) * BLK] = part
        logits_t = dot_nn(part, block_maps(wfeat_ref, group)).T
        target = kept.qft if group < 3 else kept.kft
        for head in range(BLK // HD):
            start = ((group % 3) * (BLK // HD) + head) * 2 * HD
            target[start : start + 2 * HD, :] = softmax_pair(
                logits_t[head * HD : (head + 1) * HD]
            )
    centres = []
    for group in range(3):
        part = dot_nn(normed, wqkv[:, 2 * D + group * BLK : 2 * D + (group + 1) * BLK])
        part_t = part.T
        centre = jnp.mean(part_t, 1, keepdims=True)
        centres.append(centre)
        kept.vt[group * BLK : (group + 1) * BLK, :] = (part_t - centre).astype(bfloat)
    kept.rden[...] = jnp.zeros_like(kept.rden)

    def head_step(head):
        wide = pl.ds(pl.multiple_of(head * 2 * HD, 2 * HD), 2 * HD)
        thin = pl.ds(pl.multiple_of(head * HD, HD), HD)
        keys = kept.kft[wide, :].T
        queries_t = kept.qft[wide, :]
        values_t = with_ones(kept.vt[thin, :])
        for block in range(rows // BLK):
            here = slice(block * BLK, (block + 1) * BLK)
            past = slice(0, (block + 1) * BLK)
            weights = dot_nn(keys[past], queries_t[:, here]).astype(bfloat) * mask[past, here]
            summed = dot_nn(values_t[:, past], weights)
            inverse = 1.0 / summed[HD : HD + 1]
            kept.rden[pl.ds(head, 1), here] = inverse
            kept.ot[thin, here] = summed[:HD] * inverse

    @pl.loop(0, H // 4)
    def _(group):
        for head in range(4):
            head_step(4 * group + head)

    for group in range(3):
        part = kept.ot[group * BLK : (group + 1) * BLK, :] + centres[group]
        kept.mixed[:, group * BLK : (group + 1) * BLK] = part.T.astype(bfloat)
    for load in loads[2:]:
        load.wait()
    kept.middle[...] = x[...].astype(single) + dot_nn(kept.mixed[...], wout[...])
    unit, unused = standardize(kept.middle[...])
    kept.normed_two[...] = (unit * norm_ref[2:3] + norm_ref[3:4]).astype(bfloat)
    root = 0.7978845608028654
    for tile in range(FF // D):
        cols = slice(tile * D, (tile + 1) * D)
        pre = dot_nn(kept.normed_two[...], wup[:, cols])
        square = pre * pre
        bent = jnp.tanh(pre * (root + (root * 0.044715) * square))
        half = 0.5 + 0.5 * bent
        kept.hidden[:, cols] = (pre * half).astype(bfloat)
        slope = half + (pre * (half * (1.0 - bent))) * (root + (3 * root * 0.044715) * square)
        kept.slope[:, cols] = slope.astype(bfloat)


def layer_result(kept, weights):
    result = kept.middle[...] + dot_nn(kept.hidden[...], weights[3][...])
    kept.result[...] = result.astype(bfloat)


def forward_kernel(core, *refs):
    info, norm_ref, wfeat_ref = refs[:3]
    sources, refs = refs[3:8], refs[8:]
    outs, kept, refs = Kept(*refs[:KEPT]), Kept(*refs[KEPT : 2 * KEPT]), refs[2 * KEPT :]
    x, *weights = targets = refs[:5]
    mask, sem_in, sem_out = refs[5:]

    def body():
        loads = start_loads(sources, targets, sem_in)
        forward_steps(info, x, norm_ref, wfeat_ref, weights, mask, kept, loads)
        stores = start_loads(kept[:-1], outs[:-1], sem_out)
        layer_result(kept, weights)
        last = pltpu.make_async_copy(kept.result, outs.result, sem_out.at[KEPT - 1])
        last.start()
        for store in stores:
            store.wait()
        last.wait()

    pl.when(info[0] == core)(body)


def forward_call(core, info, x, norm, wfeat, wqkv, wout, wup, wdown):
    rows = x.shape[0]
    shapes = kept_shapes(rows)
    sources = (x, wqkv, wout, wup, wdown)
    kept = pl.pallas_call(
        functools.partial(forward_kernel, core),
        out_shape=list(shapes),
        in_specs=[SMEM, VMEM, VMEM] + [HBM] * 5,
        out_specs=[HBM] * KEPT,
        scratch_shapes=scratch_like(shapes)
        + scratch_like(sources)
        + [
            pltpu.VMEM((rows, rows), bfloat),
            pltpu.SemaphoreType.DMA((5,)),
            pltpu.SemaphoreType.DMA((KEPT,)),
        ],
        compiler_params=pltpu.CompilerParams(vmem_limit_bytes=VMEM_BYTES),
        cost_estimate=cost(25),
        name="layer_forward",
    )(info, norm, wfeat, *sources)
    return Kept(*kept)


def ship(info, stage, keep, send, first, sem, shards=range(16)):
    rows = keep.shape[2]
    copies = []
    for shard in shards:
        z, y, x = shard // 4, shard // 2 % 2, shard % 2
        if first == 3:
            mine = z % 2 == info[3] % 2
            place = (z // 2, shard % 4)
        else:
            mine = (x if first == 1 else y) == info[first]
            place = (z, y if first == 1 else x)
        source = stage.at[pl.ds(shard * rows, rows)]

        @pl.when(mine)
        def _():
            pltpu.make_async_copy(source, keep.at[place], sem).start()

        @pl.when(jnp.logical_not(mine))
        def _():
            pltpu.make_async_copy(source, send.at[place], sem).start()

        copies.append(pltpu.make_async_copy(source, keep.at[place], sem))
    return copies


def place(stage, part, at, rows, first_shard=0):
    size = stage.shape[0] // 16
    part = part.astype(bfloat)
    for index in range(part.shape[0] // rows):
        start = (first_shard + index) * size + at
        stage[start : start + rows, :] = part[index * rows : (index + 1) * rows]


def halves(*sizes):
    return [jax.ShapeDtypeStruct((4, 2, rows, D), bfloat) for rows in sizes for _ in range(2)]


def stages_of(*sizes):
    return [pltpu.VMEM((16 * rows, D), bfloat) for rows in sizes]


def ff_back_steps(info, g, norm_ref, weights, kept, g_pre, outs, refs, sem_out, ready):
    wup, wdown = weights[2:]
    g_middle_o, gnorm_o, keep_a, send_a, keep_b, send_b = outs
    g_middle, gnorm, stage_a, stage_b = refs
    g_t = g[...].T
    for tile in range(FF // D):
        cols = slice(tile * D, (tile + 1) * D)
        place(stage_a, dot_nn(g_t, kept.hidden[:, cols]), tile * THIN, THIN)
    ready()
    for tile in range(FF // D):
        cols = slice(tile * D, (tile + 1) * D)
        g_hidden = dot_nt(g[...], wdown[cols, :])
        g_pre[:, cols] = (g_hidden * kept.slope[:, cols].astype(single)).astype(bfloat)
    place(stage_b, dot_tn(g_pre[...], kept.normed_two[...]), 0, WIDE)
    copies = ship(info, stage_a, keep_a, send_a, 1, sem_out.at[0])
    copies += ship(info, stage_b, keep_b, send_b, 2, sem_out.at[1])
    g_normed = dot_nt(g_pre[...], wup[...])
    unit, scale = standardize(kept.middle[...])
    gnorm[0:1, :] = jnp.sum(g_normed * unit, 0, keepdims=True)
    gnorm[1:2, :] = jnp.sum(g_normed, 0, keepdims=True)
    g_middle[...] = g[...].astype(single) + standardize_back(g_normed, unit, scale, norm_ref[2:3])
    for i, (src, dst) in enumerate(((g_middle, g_middle_o), (gnorm, gnorm_o))):
        copies.append(pltpu.make_async_copy(src, dst, sem_out.at[2 + i]))
        copies[-1].start()
    return copies


def ff_back_shapes(rows):
    return [
        jax.ShapeDtypeStruct((rows, D), single),
        jax.ShapeDtypeStruct((2, D), single),
    ]


def ff_back_kernel(core, late, *refs):
    info, norm_ref = refs[:2]
    sources, refs = refs[2:9], refs[9 + late :]
    outs, targets, refs = refs[:6], refs[6:13], refs[13:]
    g, hidden, wdown, slope, normed_two, wup, middle = targets
    g_pre, *refs, sem_in, sem_out = refs
    kept = Kept(*[None] * KEPT)._replace(
        hidden=hidden, slope=slope, normed_two=normed_two, middle=middle
    )

    def body():
        loads = start_loads(sources, targets, sem_in)

        def ready():
            for load in loads[2:]:
                load.wait()

        loads[0].wait()
        loads[1].wait()
        for copy in ff_back_steps(
            info, g, norm_ref, (None, None, wup, wdown), kept, g_pre, outs, refs, sem_out, ready
        ):
            copy.wait()

    pl.when(info[0] == core)(body)


def ff_back_call(core, info, g, norm, wdown, wup, kept, after):
    rows = g.shape[0]
    loads = (g, kept.hidden, wdown, kept.slope, kept.normed_two, wup, kept.middle)
    return pl.pallas_call(
        functools.partial(ff_back_kernel, core, len(after)),
        out_shape=ff_back_shapes(rows) + halves(WIDE, WIDE),
        in_specs=[SMEM, VMEM] + [HBM] * (7 + len(after)),
        out_specs=[HBM] * 6,
        scratch_shapes=scratch_like(loads)
        + [pltpu.VMEM((rows, FF), bfloat)]
        + scratch_like(ff_back_shapes(rows))
        + stages_of(WIDE, WIDE)
        + [pltpu.SemaphoreType.DMA((7,)), pltpu.SemaphoreType.DMA((4,))],
        compiler_params=pltpu.CompilerParams(vmem_limit_bytes=VMEM_BYTES),
        cost_estimate=cost(18),
        name="feed_forward_backward",
    )(info, norm, *loads, *after)


def turn_kernel(core, *refs):
    info, norm_ref, wfeat_ref = refs[:3]
    sources, refs = refs[3:9], refs[9 + KEPT :]
    outs, back_outs, refs = Kept(*refs[:KEPT]), refs[KEPT : KEPT + 6], refs[KEPT + 6 :]
    kept, refs = Kept(*refs[:KEPT]), refs[KEPT:]
    x, *weights, g = targets = refs[:6]
    mask, *refs, sem_in, sem_out, sem_back = refs[6:]

    def body():
        loads = start_loads(sources, targets, sem_in)
        forward_steps(info, x, norm_ref, wfeat_ref, weights, mask, kept, loads)
        mine = [
            (src, dst)
            for src, dst in zip(kept, outs)
            if src is not kept.result
            and src is not kept.hidden
            and src is not kept.slope
            and src is not kept.middle
            and src is not kept.normed_two
        ]
        copies = ff_back_steps(
            info, g, norm_ref, weights, kept, kept.slope, back_outs, refs, sem_back, lambda: None
        )
        copies += start_loads([src for src, dst in mine], [dst for src, dst in mine], sem_out)
        layer_result(kept, weights)
        copies.append(pltpu.make_async_copy(kept.result, outs.result, sem_out.at[KEPT - 1]))
        copies[-1].start()
        for copy in copies:
            copy.wait()

    pl.when(info[0] == core)(body)


def turn_call(core, info, x, g, norm, wfeat, wqkv, wout, wup, wdown, previous):
    rows = x.shape[0]
    shapes = kept_shapes(rows)
    sources = (x, wqkv, wout, wup, wdown, g)
    results = pl.pallas_call(
        functools.partial(turn_kernel, core),
        out_shape=list(shapes) + ff_back_shapes(rows) + halves(WIDE, WIDE),
        in_specs=[SMEM, VMEM, VMEM] + [HBM] * (6 + KEPT),
        out_specs=[HBM] * (KEPT + 6),
        scratch_shapes=scratch_like(shapes)
        + scratch_like(sources)
        + [pltpu.VMEM((rows, rows), bfloat)]
        + scratch_like(ff_back_shapes(rows))
        + stages_of(WIDE, WIDE)
        + [
            pltpu.SemaphoreType.DMA((6,)),
            pltpu.SemaphoreType.DMA((KEPT,)),
            pltpu.SemaphoreType.DMA((4,)),
        ],
        input_output_aliases={9 + i: i for i in range(KEPT)},
        compiler_params=pltpu.CompilerParams(vmem_limit_bytes=VMEM_BYTES),
        cost_estimate=cost(40),
        name="forward_and_backward",
    )(info, norm, wfeat, *sources, *previous)
    return Kept(*results[:KEPT]), results[KEPT:]


def mix_loads(kept):
    return kept.qft, kept.kft, kept.vt, kept.ot, kept.rden, kept.qk


def start_loads(sources, targets, sems):
    loads = [
        pltpu.make_async_copy(src, dst, sems.at[i])
        for i, (src, dst) in enumerate(zip(sources, targets))
    ]
    for load in loads:
        load.start()
    return loads


def attention_back(wfeat_ref, qft, kft, vt, ot, rden, qk, mask, gm_t, gl_t, gv_t, joined, misc):
    rows = joined.shape[0]

    def head_step(head):
        wide = pl.ds(pl.multiple_of(head * 2 * HD, 2 * HD), 2 * HD)
        thin = pl.ds(pl.multiple_of(head * HD, HD), HD)
        keys_t, queries_t = kft[wide, :], qft[wide, :]
        keys = keys_t.T
        values = with_ones(vt[thin, :]).T
        inverse = rden[pl.ds(head, 1), :]
        grad = gm_t[thin, :]
        tilt = -jnp.sum(grad * ot[thin, :], 0, keepdims=True) * inverse
        high = tilt.astype(bfloat).astype(single)
        grad = grad * inverse
        fill = jnp.zeros((14, rows), single)
        grads_t = jnp.concatenate([grad, high, tilt - high, fill], 0).astype(bfloat)
        grad_low = grads_t[:HD]
        g_query = []
        g_key = [None] * (rows // BLK)
        g_value = [None] * (rows // BLK)
        for block in range(rows // BLK):
            here = slice(block * BLK, (block + 1) * BLK)
            past = slice(0, (block + 1) * BLK)
            allowed = mask[past, here]
            weights = dot_nn(keys[past], queries_t[:, here]).astype(bfloat) * allowed
            g_weights = dot_nn(values[past], grads_t[:, here]).astype(bfloat) * allowed
            g_query.append(dot_nn(keys_t[:, past], g_weights))
            for other in range(block + 1):
                part = slice(other * BLK, (other + 1) * BLK)
                more_key = dot_nt(queries_t[:, here], g_weights[part])
                more_value = dot_nt(grad_low[:, here], weights[part])
                g_key[other] = more_key if g_key[other] is None else g_key[other] + more_key
                g_value[other] = (
                    more_value if g_value[other] is None else g_value[other] + more_value
                )
        gl_t[thin, :] = softmax_pair_back(queries_t, jnp.concatenate(g_query, 1))
        later = pl.ds(pl.multiple_of(D + head * HD, HD), HD)
        gl_t[later, :] = softmax_pair_back(keys_t, jnp.concatenate(g_key, 1))
        gv_t[thin, :] = jnp.concatenate(g_value, 1).astype(bfloat)

    @pl.loop(0, H // 4)
    def _(group):
        for head in range(4):
            head_step(4 * group + head)

    for group in range(6):
        span = slice(group * BLK, (group + 1) * BLK)
        part_t = gl_t[span, :]
        joined[:, span] = dot_nt(part_t.T, block_maps(wfeat_ref, group)).astype(bfloat)
        cross = dot_nn(part_t, qk[:, span])
        for head in range(BLK // HD):
            first = group * BLK + head * HD
            misc[first : first + HD, 0:HD] = cross[
                head * HD : (head + 1) * HD, head * HD : (head + 1) * HD
            ].astype(bfloat)
    for group in range(3):
        span = slice(group * BLK, (group + 1) * BLK)
        joined[:, 2 * D + group * BLK : 2 * D + (group + 1) * BLK] = gv_t[span, :].T


def rest_grads(stage, branch, mixed, joined, normed):
    place(stage, dot_tn(branch, mixed), 0, THIN)
    place(stage, dot_tn(joined[:, 2 * D :], normed), THIN, THIN)
    place(stage, dot_tn(joined[:, : 2 * D], normed), 2 * THIN, 2 * THIN)


def stream_back(g_middle_ref, x_ref, norm_ref, gnorm_two, joined, wqkv):
    g_normed = dot_nt(joined[...], wqkv[...])
    unit, scale = standardize(x_ref[...].astype(single))
    norm_rows = jnp.concatenate(
        [
            jnp.sum(g_normed * unit, 0, keepdims=True),
            jnp.sum(g_normed, 0, keepdims=True),
            gnorm_two,
            jnp.zeros((124, D), single),
        ],
        0,
    )
    total = g_middle_ref[...] + standardize_back(g_normed, unit, scale, norm_ref[0:1])
    return total.astype(bfloat), norm_rows.T.astype(bfloat)


def place_misc(stage, misc, turned):
    for shard in range(16):
        start = (shard + 1) * REST - 16
        for block in range(6):
            source = shard * 2 * THIN + block * 16
            lanes = slice(block * 2 * HD, block * 2 * HD + HD)
            stage[start : start + 16, lanes] = misc[source : source + 16, :HD]
            source = shard * THIN + min(block, 2) * 16
            lanes = slice(block * 2 * HD + HD, (block + 1) * 2 * HD)
            stage[start : start + 16, lanes] = turned[source : source + 16, :HD]


def mix_stream_kernel(core, *refs):
    info, norm_ref, gnorm_two_ref, wfeat_ref = refs[:4]
    sources, outs, targets, refs = refs[4:14], refs[14:18], refs[18:28], refs[28:]
    g_middle, wout, *kept, x, wqkv = targets
    mask, gm_t, gl_t, gv_t, g_stream, joined, misc, turned, sem_in, sem_out = refs
    results = g_stream, joined, misc, turned

    def body():
        loads = start_loads(sources, targets, sem_in)
        fill_mask(info, mask)
        loads[0].wait()
        loads[1].wait()
        gm_t[...] = dot_nt(wout[...], g_middle[...].astype(bfloat))
        for load in loads[2:8]:
            load.wait()
        attention_back(wfeat_ref, *kept, mask, gm_t, gl_t, gv_t, joined, misc)
        for load in loads[8:]:
            load.wait()
        g_stream[...], turned[...] = stream_back(
            g_middle, x, norm_ref, gnorm_two_ref[...], joined, wqkv
        )
        for store in start_loads(results, outs, sem_out):
            store.wait()

    pl.when(info[0] == core)(body)


def attention_scratch(rows):
    return [
        pltpu.VMEM((rows, rows), bfloat),
        pltpu.VMEM((D, rows), single),
        pltpu.VMEM((2 * D, rows), bfloat),
        pltpu.VMEM((D, rows), bfloat),
    ]


def mix_stream_call(core, info, g_middle, x, norm, gnorm_two, wfeat, wout, wqkv, kept):
    rows = x.shape[0]
    shapes = [
        jax.ShapeDtypeStruct((rows, D), bfloat),
        jax.ShapeDtypeStruct((rows, 3 * D), bfloat),
        jax.ShapeDtypeStruct((2 * D, 2 * HD), bfloat),
        jax.ShapeDtypeStruct((D, 2 * HD), bfloat),
    ]
    sources = (g_middle, wout) + mix_loads(kept) + (x, wqkv)
    return pl.pallas_call(
        functools.partial(mix_stream_kernel, core),
        out_shape=shapes,
        in_specs=[SMEM] + [VMEM] * 3 + [HBM] * 10,
        out_specs=[HBM] * 4,
        scratch_shapes=scratch_like(sources)
        + attention_scratch(rows)
        + scratch_like(shapes)
        + [pltpu.SemaphoreType.DMA((10,)), pltpu.SemaphoreType.DMA((4,))],
        compiler_params=pltpu.CompilerParams(vmem_limit_bytes=VMEM_BYTES),
        cost_estimate=cost(18),
        name="mix_backward_stream",
    )(info, norm, gnorm_two, wfeat, *sources)


def mix_grads_kernel(core, *refs):
    info, g_middle_ref = refs[:2]
    sources, (keep, send) = refs[2:7], refs[8:10]
    targets, (stage, sem_in, sem_out) = refs[10:15], refs[15:]
    mixed, joined, normed, misc, turned = targets

    def body():
        for load in start_loads(sources, targets, sem_in):
            load.wait()
        branch = g_middle_ref[...].astype(bfloat)
        rest_grads(stage, branch, mixed[...], joined, normed[...])
        place_misc(stage, misc, turned)
        for copy in ship(info, stage, keep, send, 3, sem_out):
            copy.wait()

    pl.when(info[0] == core)(body)


def rest_halves():
    return [jax.ShapeDtypeStruct((2, 4, REST, D), bfloat)] * 2


def mix_grads_call(core, info, g_middle, kept, joined, misc, turned, after):
    sources = (kept.mixed, joined, kept.normed, misc, turned)
    return pl.pallas_call(
        functools.partial(mix_grads_kernel, core),
        out_shape=rest_halves(),
        in_specs=[SMEM, VMEM] + [HBM] * 6,
        out_specs=[HBM] * 2,
        scratch_shapes=scratch_like(sources)
        + stages_of(REST)
        + [pltpu.SemaphoreType.DMA((5,)), pltpu.SemaphoreType.DMA],
        compiler_params=pltpu.CompilerParams(vmem_limit_bytes=VMEM_BYTES),
        cost_estimate=cost(0.1),
        name="mix_backward_gradients",
    )(info, g_middle, *sources, after)


def mix_back_kernel(core, late, *refs):
    info, norm_ref, gnorm_two_ref, wfeat_ref = refs[:4]
    sources, refs = refs[4:16], refs[17 + late :]
    g_stream_o, keep, send = refs[:3]
    targets, refs = refs[3:15], refs[15:]
    g_middle, wout, *kept, x, mixed, normed, wqkv = targets
    mask, gm_t, gl_t, gv_t, joined, misc, g_stream, stage, sem_in, sem_out = refs

    def body():
        loads = start_loads(sources, targets, sem_in)
        fill_mask(info, mask)
        loads[0].wait()
        loads[1].wait()
        branch = g_middle[...].astype(bfloat)
        gm_t[...] = dot_nt(wout[...], branch)
        for load in loads[2:8]:
            load.wait()
        attention_back(wfeat_ref, *kept, mask, gm_t, gl_t, gv_t, joined, misc)
        for load in loads[8:]:
            load.wait()
        rest_grads(stage, branch, mixed[...], joined, normed[...])
        g_stream[...], turned = stream_back(
            g_middle, x, norm_ref, gnorm_two_ref[...], joined, wqkv
        )
        place_misc(stage, misc, turned)
        copies = ship(info, stage, keep, send, 1, sem_out.at[0])
        copies.append(pltpu.make_async_copy(g_stream, g_stream_o, sem_out.at[1]))
        copies[-1].start()
        for copy in copies:
            copy.wait()

    pl.when(info[0] == core)(body)


def mix_back_call(
    core, info, g_middle, x, norm, gnorm_two, wfeat, wout, wqkv, kept, previous, after
):
    rows = x.shape[0]
    shapes = [jax.ShapeDtypeStruct((rows, D), bfloat)] + halves(REST)
    sources = (g_middle, wout) + mix_loads(kept) + (x, kept.mixed, kept.normed, wqkv)
    return pl.pallas_call(
        functools.partial(mix_back_kernel, core, len(after)),
        out_shape=shapes,
        in_specs=[SMEM] + [VMEM] * 3 + [HBM] * (13 + len(after)),
        out_specs=[HBM] * 3,
        scratch_shapes=scratch_like(sources)
        + attention_scratch(rows)
        + [
            pltpu.VMEM((rows, 3 * D), bfloat),
            pltpu.VMEM((2 * D, 2 * HD), bfloat),
            pltpu.VMEM((rows, D), bfloat),
        ]
        + stages_of(REST)
        + [pltpu.SemaphoreType.DMA((12,)), pltpu.SemaphoreType.DMA((2,))],
        input_output_aliases={16: 0},
        compiler_params=pltpu.CompilerParams(vmem_limit_bytes=VMEM_BYTES),
        cost_estimate=cost(22),
        name="mix_backward",
    )(info, norm, gnorm_two, wfeat, *sources, previous, *after)


class Travel(NamedTuple):
    keep_a: Any
    one_a: Any
    keep_b: Any = None
    one_b: Any = None
    two_a: Any = None
    two_b: Any = None
    low: Any = None
    high: Any = None


def rows_of(travel):
    return sum(keep.shape[2] for keep in (travel.keep_a, travel.keep_b) if keep is not None)


def at_shard(travel, z, x, y, z_high):
    rows_a, rows = travel.keep_a.shape[2], rows_of(travel)
    pieces = [(travel.keep_a, travel.one_a, travel.two_a, y, pl.ds(0, rows_a))]
    if travel.keep_b is not None:
        pieces.append((travel.keep_b, travel.one_b, travel.two_b, x, pl.ds(rows_a, rows - rows_a)))
    terms = [
        [(keep.at[z, index], span) for keep, one, two, index, span in pieces],
        [(one.at[z, index], span) for keep, one, two, index, span in pieces],
    ]
    if travel.two_a is not None:
        terms.append([(two.at[z], span) for keep, one, two, index, span in pieces])
    if travel.low is not None:
        terms.append([(travel.low.at[z_high], pl.ds(0, rows))])
    if travel.high is not None:
        terms.append([(travel.high, pl.ds(0, rows))])
    return terms


def packed(travel):
    there = [value is not None for value in travel]

    def unpack(refs):
        refs = iter(refs)
        return type(travel)(*[next(refs) if here else None for here in there])

    return [value for value in travel if value is not None], unpack


def fetch(terms, held, sems):
    copies = []
    for index, pieces in enumerate(terms):
        for piece, (source, span) in enumerate(pieces):
            copies.append(
                pltpu.make_async_copy(source, held.at[index, span], sems.at[index, piece])
            )
    for copy in copies:
        copy.start()
    return copies


def total_of(held, count):
    total = held[0].astype(single)
    for index in range(1, count):
        total = total + held[index].astype(single)
    return total


def second_hop_kernel(core, count, info, *refs):
    travel, refs = refs[: 2 * count], refs[2 * count + 1 :]
    outs, held, more = refs[:count], refs[count : 2 * count], refs[2 * count : 3 * count]
    sem_in, sem_out = refs[3 * count :]

    def body():
        x, y = info[1], info[2]
        copies = []
        for i in range(count):
            other = 1 - (x if i else y)
            for j, target in enumerate((held[i], more[i])):
                source = travel[2 * i + j].at[:, other]
                copies.append(pltpu.make_async_copy(source, target, sem_in.at[2 * i + j]))
        for copy in copies:
            copy.start()
        stores = []
        for i in range(count):
            copies[2 * i].wait()
            copies[2 * i + 1].wait()
            total = held[i][...].astype(single) + more[i][...].astype(single)
            held[i][...] = total.astype(bfloat)
            stores.append(pltpu.make_async_copy(held[i], outs[i], sem_out.at[i]))
            stores[-1].start()
        for store in stores:
            store.wait()

    pl.when(info[0] == core)(body)


def second_hop_call(core, info, travel, after):
    refs = [value for value in travel[:4] if value is not None]
    count = len(refs) // 2
    shapes = [jax.ShapeDtypeStruct((4,) + keep.shape[2:], bfloat) for keep in refs[::2]]
    return pl.pallas_call(
        functools.partial(second_hop_kernel, core, count),
        out_shape=shapes,
        in_specs=[SMEM] + [HBM] * (2 * count + 1),
        out_specs=[HBM] * count,
        scratch_shapes=scratch_like(shapes * 2)
        + [pltpu.SemaphoreType.DMA((2 * count,)), pltpu.SemaphoreType.DMA((count,))],
        compiler_params=pltpu.CompilerParams(vmem_limit_bytes=VMEM_BYTES),
        cost_estimate=cost(0.1),
        name="for_second_hop",
    )(info, *refs, after)


def z_hop_kernel(core, count, unpack, info, *refs):
    travel, refs = unpack(refs[:count]), refs[count + 1 :]
    out, held, total, sem_in, sem_out = refs

    def body():
        x, y, z = info[1], info[2], info[3]
        low, high = z % 2, z // 2
        if travel.low is None:
            targets = [((1 - low), 0), (2 + (1 - low), 1)]
        else:
            targets = [(2 * (1 - high) + low, 1 - high)]
        copies = [
            fetch(at_shard(travel, target, x, y, target_high), held.at[index], sem_in.at[index])
            for index, (target, target_high) in enumerate(targets)
        ]
        stores = []
        for index in range(len(targets)):
            for copy in copies[index]:
                copy.wait()
            count_terms = 3 if travel.low is None else 4
            total[index] = total_of(held.at[index], count_terms).astype(bfloat)
            to = out.at[index] if travel.low is None else out
            stores.append(pltpu.make_async_copy(total.at[index], to, sem_out.at[index]))
            stores[-1].start()
        for store in stores:
            store.wait()

    pl.when(info[0] == core)(body)


def z_hop_call(core, info, travel, after):
    rows = rows_of(travel)
    refs, unpack = packed(travel)
    shape = (2, rows, D) if travel.low is None else (rows, D)
    return pl.pallas_call(
        functools.partial(z_hop_kernel, core, len(refs), unpack),
        out_shape=jax.ShapeDtypeStruct(shape, bfloat),
        in_specs=[SMEM] + [HBM] * (len(refs) + 1),
        out_specs=HBM,
        scratch_shapes=[
            pltpu.VMEM((2, 4, rows, D), bfloat),
            pltpu.VMEM((2, rows, D), bfloat),
            pltpu.SemaphoreType.DMA((2, 4, 2)),
            pltpu.SemaphoreType.DMA((2,)),
        ],
        compiler_params=pltpu.CompilerParams(vmem_limit_bytes=VMEM_BYTES),
        cost_estimate=cost(0.1),
        name="for_z_hop",
    )(info, *refs, after)


def finish_kernel(counts, unpacks, write, info, *refs):
    travels = unpacks[0](refs[: counts[0]]), unpacks[1](refs[counts[0] : sum(counts)])
    outs = refs[sum(counts) : -2]
    held, sem_in = refs[-2:]

    def bring(travel):
        x, y, z = info[1], info[2], info[3]
        if isinstance(travel, Travel):
            terms = at_shard(travel, z, x, y, z // 2)
        else:
            terms = rest_at(travel, x, y, z // 2)
        for copy in fetch(terms, held, sem_in):
            copy.wait()

    for core in range(2):
        pl.when(info[0] == core)(functools.partial(bring, travels[core]))
    write(total_of(held, 5), outs)


def write_early(total, outs):
    down, up = outs
    for tile in range(FF // D):
        down[0, :, tile * D : (tile + 1) * D] = total[tile * THIN : (tile + 1) * THIN]
    up[0] = total[WIDE:]


def write_rest(total, outs):
    norms, pairs, value, maps, out = outs
    out[0] = total[:THIN]
    value[0] = total[THIN : 2 * THIN]
    pairs[0] = total[2 * THIN : 4 * THIN]
    misc = total[4 * THIN :]
    tall = [misc[:, i * 2 * HD : (i + 1) * 2 * HD] for i in range(6)]
    wide = jnp.concatenate(tall + [jnp.zeros((32, 2 * HD), single)], 0).T
    maps[0] = wide[:HD, : 2 * THIN]
    norms[0] = wide[HD : HD + 4, :THIN]


def finish_call(info, first, second, rows, shapes, write):
    (first, unpack_first), (second, unpack_second) = packed(first), packed(second)
    counts = len(first), len(second)
    return pl.pallas_call(
        functools.partial(finish_kernel, counts, (unpack_first, unpack_second), write),
        out_shape=[jax.ShapeDtypeStruct((1,) + shape, single) for shape in shapes],
        in_specs=[SMEM] + [HBM] * sum(counts),
        out_specs=[VMEM] * len(shapes),
        scratch_shapes=[
            pltpu.VMEM((5, rows, D), bfloat),
            pltpu.SemaphoreType.DMA((5, 2)),
        ],
        compiler_params=pltpu.CompilerParams(vmem_limit_bytes=VMEM_BYTES),
        cost_estimate=cost(0.1),
        name="shard_gradients",
    )(info, *first, *second)


class RestTravel(NamedTuple):
    keep: Any
    low: Any = None
    high: Any = None
    x: Any = None
    y: Any = None


def rest_at(travel, x, y, z_high):
    terms = [travel.keep.at[z_high, 2 * y + x], travel.low.at[z_high, 2 * y + x]]
    if travel.high is not None:
        terms.append(travel.high.at[2 * y + x])
    if travel.x is not None:
        terms.append(travel.x.at[y])
    if travel.y is not None:
        terms.append(travel.y)
    return [((term, pl.ds(0, REST)),) for term in terms]


def rest_hop_kernel(core, count, info, *refs):
    travel, refs = RestTravel(*refs[:count]), refs[count + 1 :]
    out, held, total, sem_in, sem_out = refs

    def body():
        x, y, z_high = info[1], info[2], info[3] // 2
        if count == 2:
            targets = [(i % 2, i // 2, 1 - z_high) for i in range(4)]
        elif count == 3:
            targets = [(1 - x, i, z_high) for i in range(2)]
        else:
            targets = [(x, 1 - y, z_high)]
        copies = [
            fetch(rest_at(travel, *target), held.at[i], sem_in.at[i])
            for i, target in enumerate(targets)
        ]
        stores = []
        for i in range(len(targets)):
            for copy in copies[i]:
                copy.wait()
            total[i] = total_of(held.at[i], count).astype(bfloat)
            to = out if len(targets) == 1 else out.at[i]
            stores.append(pltpu.make_async_copy(total.at[i], to, sem_out.at[i]))
            stores[-1].start()
        for store in stores:
            store.wait()

    pl.when(info[0] == core)(body)


def rest_hop_call(core, info, travel, after):
    refs = [ref for ref in travel if ref is not None]
    many = {2: 4, 3: 2, 4: 1}[len(refs)]
    shape = (REST, D) if many == 1 else (many, REST, D)
    return pl.pallas_call(
        functools.partial(rest_hop_kernel, core, len(refs)),
        out_shape=jax.ShapeDtypeStruct(shape, bfloat),
        in_specs=[SMEM] + [HBM] * (len(refs) + 1),
        out_specs=HBM,
        scratch_shapes=[
            pltpu.VMEM((many, len(refs), REST, D), bfloat),
            pltpu.VMEM((many, REST, D), bfloat),
            pltpu.SemaphoreType.DMA((many, len(refs), 1)),
            pltpu.SemaphoreType.DMA((many,)),
        ],
        compiler_params=pltpu.CompilerParams(vmem_limit_bytes=VMEM_BYTES),
        cost_estimate=cost(0.1),
        name="for_rest_hop",
    )(info, *refs, after)


def swap_on(value, core, axis, bit):
    count = lax.axis_size(axis)
    pairs = [(core * count + i, core * count + (i ^ bit)) for i in range(count)]
    return lax.ppermute(value, ("pipe", axis), pairs)


def fast_on_device(
    tokens,
    cotangent,
    lengths,
    norm_params,
    qkv_weight,
    feature_weight,
    out_weight,
    up_weight,
    down_weight,
):
    norm, wqkv, wfeat = norm_params[0], qkv_weight[0], feature_weight[0]
    wout, wup, wdown = out_weight[0], up_weight[0], down_weight[0]
    pipe, seq = lax.axis_index("pipe"), lax.axis_index("seq")
    ends = jnp.cumsum(lax.dynamic_index_in_dim(lengths, seq, 0, False)).astype(jnp.int32)
    places = jnp.stack([pipe, seq % 2, seq // 2, lax.axis_index("dp")]).astype(jnp.int32)
    info = jnp.concatenate([places, ends])
    whole = lax.all_to_all(tokens, "seq", 0, 0, tiled=True).reshape(-1, D)
    whole_grad = lax.all_to_all(cotangent, "seq", 0, 0, tiled=True).reshape(-1, D)

    def one(core, parts):
        keep_a, send_a, *piece_b = parts
        travel = Travel(keep_a, swap_on(send_a, core, "seq", 1))
        if piece_b:
            travel = travel._replace(keep_b=piece_b[0], one_b=swap_on(piece_b[1], core, "seq", 2))
        return travel

    def two(core, travel, after):
        send_a, *send_b = second_hop_call(core, info, travel, after)
        travel = travel._replace(two_a=swap_on(send_a, core, "seq", 2))
        if send_b:
            travel = travel._replace(two_b=swap_on(send_b[0], core, "seq", 1))
        return send_a, travel

    def low(core, travel, after):
        send = z_hop_call(core, info, travel, after)
        return send, travel._replace(low=swap_on(send, core, "dp", 1))

    def high(core, travel, after):
        send = z_hop_call(core, info, travel, after)
        return send, travel._replace(high=swap_on(send, core, "dp", 2))

    def rest_low(core, parts):
        keep, send = parts
        return RestTravel(keep, swap_on(send, core, "dp", 1))

    def rest_high(core, travel, after):
        send = rest_hop_call(core, info, travel, after)
        return send, travel._replace(high=swap_on(send, core, "dp", 2))

    def rest_x(core, travel, after):
        send = rest_hop_call(core, info, travel, after)
        return send, travel._replace(x=swap_on(send, core, "seq", 1))

    def rest_y(core, travel, after):
        send = rest_hop_call(core, info, travel, after)
        return send, travel._replace(y=swap_on(send, core, "seq", 2))

    def back_to_rows(value):
        return lax.all_to_all(value.reshape(tokens.shape), "seq", 0, 0, tiled=True)[None]

    kept = forward_call(0, info, whole, norm, wfeat, wqkv, wout, wup, wdown)
    sent = lax.ppermute(kept.result, "pipe", [(0, 1)])
    kept, (g_middle, gnorm_two, *parts) = turn_call(
        1, info, sent, whole_grad, norm, wfeat, wqkv, wout, wup, wdown, kept
    )
    early_one = one(1, parts)
    g_stream, joined, misc, turned = mix_stream_call(
        1, info, g_middle, sent, norm, gnorm_two, wfeat, wout, wqkv, kept
    )
    returned = lax.ppermute(g_stream, "pipe", [(1, 0)])
    last, early_one = two(1, early_one, g_stream)
    parts = mix_grads_call(1, info, g_middle, kept, joined, misc, turned, last)
    rest_one = rest_low(1, parts)

    layer_out = back_to_rows(kept.result)
    g_middle, gnorm_two, *parts = ff_back_call(
        0, info, returned, norm, wdown, wup, kept, (parts[0], layer_out)
    )
    early_two = one(0, parts)
    last = g_middle
    last, early_one = low(1, early_one, last)
    g_stream, *parts = mix_back_call(
        0, info, g_middle, whole, norm, gnorm_two, wfeat, wout, wqkv, kept, g_stream, (last,)
    )
    rest_two = one(0, parts)
    last = g_stream
    last, early_two = two(0, early_two, last)
    last, rest_one = rest_high(1, rest_one, last)
    last, rest_two = two(0, rest_two, last)
    last, early_two = low(0, early_two, last)
    last, rest_two = low(0, rest_two, last)
    last, early_one = high(1, early_one, last)
    last, rest_one = rest_x(1, rest_one, last)
    last, early_two = high(0, early_two, last)
    last, rest_two = high(0, rest_two, last)
    last, rest_one = rest_y(1, rest_one, last)
    input_grad = back_to_rows(g_stream)
    down, up = finish_call(
        info, early_two, early_one, 2 * WIDE, [(THIN, FF), (WIDE, D)], write_early
    )
    norms, pairs, value, maps, out = finish_call(
        info,
        rest_two,
        rest_one,
        REST,
        [(4, THIN), (2 * THIN, D), (THIN, D), (HD, 2 * THIN), (THIN, D)],
        write_rest,
    )
    down, up, pairs, value, out = [g.swapaxes(1, 2) for g in (down, up, pairs, value, out)]

    return layer_out, input_grad, norms, pairs, value, maps, out, up, down


def on_device(tokens, cotangent, lengths, *params):
    suits = (lax.axis_size("dp"), lax.axis_size("seq"), tokens.shape[0]) == (4, 4, 4)
    plan = fast_on_device if suits else general_on_device
    return plan(tokens, cotangent, lengths, *params)


def solution(mesh):
    in_specs = (
        P("dp", "seq", None),
        P("dp", "seq", None),
        P("dp", None),
        P("pipe", None, None),
        P("pipe", None, None),
        P("pipe", None, None),
        P("pipe", None, None),
        P("pipe", None, None),
        P("pipe", None, None),
    )
    out_specs = (
        P("pipe", "dp", "seq", None),
        P("pipe", "dp", "seq", None),
        P("pipe", None, ("dp", "seq")),
        P("pipe", None, ("dp", "seq")),
        P("pipe", None, ("dp", "seq")),
        P("pipe", None, ("dp", "seq")),
        P("pipe", None, ("dp", "seq")),
        P("pipe", None, ("dp", "seq")),
        P("pipe", None, ("dp", "seq")),
    )
    return jax.shard_map(
        on_device, mesh=mesh, in_specs=in_specs, out_specs=out_specs, check_vma=False
    )
```
